512 devices in a mesh: grp: 32 (over z, x), slc: 16 (over y, core).
Axes of the slice: x: 4, y: 8, z: 8, core: 2. Of those that a mesh axis runs over, the one named last changes fastest.
Arguments:
- orbitals: float32 [1024, 48, 2304], P('grp', 'slc'), may hold values from -6 to 6
- local_pot: float32 [1024, 48, 2304], P('grp', 'slc'), may hold values from -1 to 1
- pair_owner: int32 [32, 32, 1], P('grp'), may hold values from 0 to 31; in each aligned block of 32 rows (0 to 31, 32 to 63, ..., all dimensions but the last counted through in order) at most 2 rows name the same one
- pair_remote: int32 [32, 32], P('grp'), may hold values from 0 to 31
- pair_resident: int32 [32, 32], P('grp'), may hold values from 0 to 1
- pair_count: int32 [32, 16], P('grp'), may hold values from 1 to 3, 32 in all within a row
- offsets: int32 [1024, 3], replicated, may hold values from 0 to 23
Outputs:
- applied: float32 [1024, 48, 2304], P('grp', 'slc')
The draws below stay inside these ranges and needn't reach their ends.
Inputs may be any that keep to these rules, and one draw needn't show every extreme that they name: `pair_owner`: within one group's 32 pairs no owner group is named more than 2 times, and some owner group is named exactly 2 times. `pair_count`: the 16 counts of one group sum to 32, and in every group some device has exactly 3.
All inputs are finite; a program needn't handle non-finite values.
Results may differ from the reference program's by a relative error of at most 0.0003.
Values sent between devices are 32-bit elements; how exact they have to be, the bound alone decides.
A program may use at most 128 MiB of HBM per device.

```python
import math
import jax
import jax.numpy as jnp
import numpy as np
from jax import lax

B = 48
ORB_DEV = 2
PAIRS = 3
LIVE_GRP = 32
CAP = 2
SPREAD = 24
ORB_GRP = 32
ORBITALS = 1024
N_GRP = 32
N_SLC = 16


def touch_ends(values, rng, least, top_value):
    index_at = [jax.random.randint(jax.random.fold_in(rng, axis), (), 0, length) for axis, length in enumerate(values.shape)]
    widest = values.shape.index(max(values.shape))
    beside = index_at[:widest] + [(index_at[widest] + 1) % values.shape[widest]] + index_at[widest + 1:]
    return values.at[tuple(index_at)].set(least).at[tuple(beside)].set(top_value)


def shard_levels(rng, shape, pieces, least, top_value):
    factor_of, own = 1.0, jax.random.fold_in(rng, 6)
    for dim, blocks in pieces:
        draws = jnp.exp(jax.random.uniform(jax.random.fold_in(own, dim), (blocks,), jnp.float32, least / len(pieces), top_value / len(pieces)))
        factor_of = factor_of * jnp.repeat(draws, shape[dim] // blocks).reshape([-1 if axis == dim else 1 for axis in range(len(shape))])
    return factor_of


def split_up(count, total, reach, lean):
    weights = [(1 << 20) // math.isqrt(standing ** lean) + 1 for standing in range(2, count + 1)]
    rest, given = total - reach - (count - 1), [1] * (count - 1)
    while rest > 0:
        candidates = [i for i in range(count - 1) if given[i] < reach]
        mass, remaining = sum([weights[i] for i in candidates]), rest
        for i in candidates:
            more = min(reach - given[i], max(1, remaining * weights[i] // mass), rest)
            given[i] = given[i] + more
            rest = rest - more
    return np.array([reach] + given)


def ragged_sizes(key, number_of, total, reach, lean):
    if number_of == 2:
        one = jax.random.randint(key, (), max(1, total - reach), min(reach, total - 1) + 1)
        return jnp.stack([one, total - one])
    sizes = jnp.asarray(split_up(number_of, total, reach, lean), jnp.int32)
    pairs = (number_of - 1) // 2
    giver, sink = sizes[1:1 + 2 * pairs:2], sizes[2:2 + 2 * pairs:2]
    slack = jnp.minimum(giver - 1, reach - sink)
    moved = jax.random.randint(jax.random.fold_in(key, 1), (pairs,), 0, 1 << 20) % (slack + 1)
    sizes = sizes.at[1:1 + 2 * pairs:2].set(giver - moved).at[2:2 + 2 * pairs:2].set(sink + moved)
    return sizes[jax.random.permutation(jax.random.fold_in(key, 2), number_of)]


def deal_out(rng, own, number, rows, count, top, bound, skew):
    sequence = jax.random.permutation(rng, count)
    crowded, common = portions_of(count, rows * top, bound, skew, True), portions_of(count, rows * top, bound, skew, False)
    places = jnp.arange(count)

    def named(sizes, turn):
        used = int((sizes > 0).sum())
        fixed = max(1, used // 4)
        moved = fixed + (places - fixed + turn * (used - fixed)) % max(1, count - fixed)
        return jnp.zeros((count,), jnp.int32).at[sequence[jnp.where(places < fixed, places, moved)]].set(jnp.asarray(sizes, jnp.int32))

    sizes = jnp.where(number % 4 == 0, named(crowded, number // 4), named(common, number - number // 4 - 1))
    mixed = jax.random.permutation(jax.random.fold_in(own, 3), count)
    source_of, taker = mixed[0:count // 2 * 2:2], mixed[1:count // 2 * 2:2]
    room = jnp.minimum(sizes[source_of] - 1, bound - sizes[taker]) // 2
    room = jnp.where((source_of == sequence[0]) | (taker == sequence[0]) | (sizes[taker] == 0), 0, jnp.maximum(room, 0))
    moved = jax.random.randint(jax.random.fold_in(own, 4), (count // 2,), 0, 1 << 20) % (room + 1)
    sizes = sizes.at[source_of].add(-moved).at[taker].add(moved)
    items = jnp.searchsorted(jnp.cumsum(sizes), jnp.arange(rows * top), side="right").astype(jnp.int32)
    listing = items.reshape(top, rows).T
    listing = listing[jax.random.permutation(jax.random.fold_in(own, 1), rows)]
    turn = jax.random.randint(jax.random.fold_in(own, 2), (rows, 1), 0, top)
    return jnp.take_along_axis(listing, (jnp.arange(top)[None, :] + turn) % top, axis=1)


def portions_of(number_of, total, reach, lean, full):
    portions = [(1 << 20) // math.isqrt(standing ** lean) + 1 for standing in range(1, number_of + 1)]
    largest = reach if full else min(reach, max(-(-total // number_of), total * portions[0] // sum(portions)))
    least = 1 if total - largest >= number_of - 1 else 0
    holding, rest = [largest] + [least] * (number_of - 1), total - largest - least * (number_of - 1)
    while rest > 0:
        movable = [i for i in range(1, number_of) if holding[i] < largest] or [i for i in range(1, number_of) if holding[i] < reach]
        whole, left = sum([portions[i] for i in movable]), rest
        for i in movable:
            more = min(reach - holding[i], max(1, left * portions[i] // whole), rest)
            holding[i] = holding[i] + more
            rest = rest - more
    return np.array(holding)


def scatter_about(key, extent, scale, most, pieces=(), kind=jnp.bfloat16):
    level = shard_levels(key, extent, pieces, -0.22, 0.18) if pieces else 1.0
    values = jax.random.normal(key, extent, jnp.float32) * scale * level
    return jnp.minimum(jnp.maximum(values, -most), most).astype(kind)


def setup_inputs(seed: int = 0) -> dict:
    key_of = jax.random.split(jax.random.key(seed), 8)
    orbitals = scatter_about(key_of[0], (ORBITALS, B, B * B), 1.0, 6.0, ((0, 32), (1, 16)), jnp.float32)
    local_pot = jnp.clip(jax.random.uniform(key_of[1], (ORBITALS, B, B * B), jnp.float32, -1.0, 1.0) * shard_levels(key_of[1], (ORBITALS, B, B * B), ((0, 32), (1, 16)), -0.4, 0.0), -1.0, 1.0)
    pair_owner_keys = jax.random.split(jax.random.fold_in(key_of[2], 1), N_GRP * LIVE_GRP // LIVE_GRP)
    pair_owner_turns = jax.random.permutation(jax.random.fold_in(key_of[2], 3), N_GRP * LIVE_GRP // LIVE_GRP)
    pair_owner = jax.vmap(lambda own, number: deal_out(jax.random.fold_in(key_of[2], 2), own, number, LIVE_GRP, N_GRP, 1, CAP, 2))(pair_owner_keys, pair_owner_turns).reshape((N_GRP, LIVE_GRP, 1))
    pair_remote = touch_ends(jax.random.randint(key_of[3], (N_GRP, LIVE_GRP), 0, ORB_GRP), jax.random.fold_in(key_of[3], 1), 0, ORB_GRP - 1).astype(jnp.int32)
    pair_resident = touch_ends(jax.random.randint(key_of[4], (N_GRP, LIVE_GRP), 0, ORB_DEV), jax.random.fold_in(key_of[4], 1), 0, ORB_DEV - 1).astype(jnp.int32)
    pair_count = jax.vmap(lambda own: ragged_sizes(own, N_SLC, LIVE_GRP, PAIRS, 2))(jax.random.split(key_of[5], N_GRP)).reshape((N_GRP, N_SLC)).astype(jnp.int32)
    offsets = touch_ends(jax.random.randint(key_of[6], (ORBITALS, 3), 0, SPREAD), jax.random.fold_in(key_of[6], 1), 0, SPREAD - 1).astype(jnp.int32)
    return {"orbitals": orbitals, "local_pot": local_pot, "pair_owner": pair_owner, "pair_remote": pair_remote, "pair_resident": pair_resident, "pair_count": pair_count, "offsets": offsets}


highest = lax.Precision.HIGHEST
coupling = 1.0

def sine_table(box_edge):
    positions = jnp.arange(box_edge, dtype=jnp.float32)
    phases = jnp.pi * (positions[:, None] + 1.0) * (positions[None, :] + 1.0) / (box_edge + 1.0)
    return jnp.sqrt(2.0 / (box_edge + 1.0)) * jnp.sin(phases)

def kernel_weights(box_edge):
    positions = jnp.arange(box_edge, dtype=jnp.float32)
    eigenvalues = 2.0 - 2.0 * jnp.cos(jnp.pi * (positions + 1.0) / (box_edge + 1.0))
    return coupling / (eigenvalues[:, None, None] + eigenvalues[None, :, None] + eigenvalues[None, None, :])

def shift_matrix(amount, box_edge):
    positions = jnp.arange(box_edge, dtype=jnp.int32)
    return (positions[None, :] == positions[:, None] + amount).astype(jnp.float32)

def three_ways(mat_first, mat_second, mat_third, box_values):
    box_values = jnp.einsum('ka,abc->bck', mat_first, box_values, precision=highest)
    box_values = jnp.einsum('ka,abc->bck', mat_second, box_values, precision=highest)
    return jnp.einsum('ka,abc->bck', mat_third, box_values, precision=highest)

def one_pair(resident_box, partner_box, offset_gap, sine_rows, weights):
    box_edge = resident_box.shape[0]
    shift_first = shift_matrix(offset_gap[0], box_edge)
    shift_second = shift_matrix(offset_gap[1], box_edge)
    shift_third = shift_matrix(offset_gap[2], box_edge)
    shifted = three_ways(shift_first, shift_second, shift_third, partner_box)
    density = resident_box * shifted
    spectrum = three_ways(sine_rows, sine_rows, sine_rows, density)
    potential = three_ways(sine_rows, sine_rows, sine_rows, weights * spectrum)
    near_field = potential * shifted
    far_field = three_ways(shift_first.T, shift_second.T, shift_third.T, potential * resident_box)
    return (near_field, far_field)

def reference(orbitals, local_pot, pair_owner, pair_remote, pair_resident, pair_count, offsets):
    orbital_boxes = orbitals.reshape(ORBITALS, B, B, B)
    place = jnp.arange(LIVE_GRP, dtype=jnp.int32)
    running = jnp.cumsum(pair_count.astype(jnp.int32), axis=1)
    device_of = lax.optimization_barrier(jnp.sum((running[:, None, :] <= place[None, :, None]).astype(jnp.int32), axis=2))
    group_of = jnp.arange(N_GRP, dtype=jnp.int32)[:, None] + jnp.zeros((1, LIVE_GRP), jnp.int32)
    resident = (group_of * ORB_GRP + device_of * ORB_DEV + pair_resident.astype(jnp.int32)).reshape(-1)
    partner = (pair_owner[:, :, 0].astype(jnp.int32) * ORB_GRP + pair_remote.astype(jnp.int32)).reshape(-1)
    offset_gaps = jnp.take(offsets, resident, axis=0) - jnp.take(offsets, partner, axis=0)
    sine_rows = sine_table(B)
    weights = kernel_weights(B)

    def pair_step(fields, scan_item):
        near_index, far_index, offset_gap = scan_item
        near_field, far_field = one_pair(orbital_boxes[near_index], orbital_boxes[far_index], offset_gap, sine_rows, weights)
        fields = fields.at[near_index].add(near_field)
        fields = fields.at[far_index].add(far_field)
        return (fields, None)
    start = jnp.zeros((ORBITALS, B, B, B), jnp.float32)
    fields, unused = lax.scan(pair_step, start, (resident, partner, offset_gaps))
    return local_pot * orbitals - fields.reshape(orbitals.shape)
```

```python
import functools

import jax
import jax.numpy as jnp
import numpy as np
from jax import lax
from jax.experimental import pallas as pl
from jax.experimental.pallas import tpu as pltpu
from jax.sharding import PartitionSpec as P

B = 48
CELLS = B * B
LANES = 128
BLOCKS = CELLS // LANES
PLANES = 3
ROWS = 56
GRP = 32
SLC = 16
ORB = 32
CAP = 2
LIVE = 2
CHUNKS = ((0, 24), (24, 16), (40, 16))
WIDE = 384
VMEM_LIMIT = 48 * 1024 * 1024


def split_np(values):
    high = values.astype(jnp.bfloat16)
    low = (values - high.astype(np.float64)).astype(jnp.bfloat16)
    return high, low


@functools.cache
def tables():
    k = np.arange(B, dtype=np.float64)
    q = np.sqrt(2.0 / (B + 1)) * np.sin(np.pi * np.outer(k + 1, k + 1) / (B + 1))
    lam = 2.0 - 2.0 * np.cos(np.pi * (k + 1) / (B + 1))
    plane_of = 3 * (np.arange(B) % SLC) + np.arange(B) // SLC
    q_c = np.kron(np.eye(WIDE // B), q)
    q_a = np.zeros((2 * B, LANES))
    for p in range(2):
        q_a[p * B : (p + 1) * B, p * B : (p + 1) * B] = q[plane_of]
    q_high, q_low = split_np(q)
    q_b = np.concatenate([q_high, q_low, q_high], axis=1)
    lam_b = np.broadcast_to(lam[:, None], (B, LANES)).astype(np.float32)
    lane = np.arange(LANES)
    lam_a = np.where(lane < 2 * B, lam[lane % B], 1.0)
    lam_ac = np.zeros((B // 2, 1, 2 * LANES), np.float32)
    for kc in range(B):
        lam_ac[kc // 2, 0, (kc % 2) * LANES : (kc % 2 + 1) * LANES] = lam_a + lam[kc]
    return (*split_np(q_c), *split_np(q_a), q_b, lam_b, lam_ac)


def turn_of(i):
    return (i // 2 + 1) * (1 - 2 * (i % 2))


def peer(me, i, count):
    return lax.rem(me + turn_of(i) + count, count)


def greet_all(me_g, me_s):
    barrier = pltpu.get_barrier_semaphore()

    def greet_grp(i, _):
        pl.semaphore_signal(barrier, inc=1, device_id={"grp": peer(me_g, i, GRP)})
        return 0

    def greet_slc(i, _):
        pl.semaphore_signal(barrier, inc=1, device_id={"slc": peer(me_s, i, SLC)})
        return 0

    lax.fori_loop(0, GRP - 1, greet_grp, 0)
    lax.fori_loop(0, SLC - 1, greet_slc, 0)
    return barrier


def fetch_kernel(
    near_idx, far_slot, own_want, orb, want,
    near_box, far_box, req_out,
    slabs, near_send, req_recv, req_smem,
    gs0, gs1, gs2, gr0, gr1, gr2, fs0, fs1, fs2,
    rq_send, rq_recv, n_send, n_recv, g_send, g_recv, f_send, f_recv, loc_sem,
):
    me_g = lax.axis_index("grp")
    me_s = lax.axis_index("slc")
    barrier = greet_all(me_g, me_s)
    for q in range(BLOCKS):
        slabs[:ORB, 3 * q : 3 * q + 3, :] = orb[:, :, q * LANES : (q + 1) * LANES]
    slabs[:ORB, 54:56, :] = jnp.zeros((ORB, 2, LANES), jnp.float32)
    slabs[ORB] = jnp.zeros((ROWS, LANES), jnp.float32)
    pl.semaphore_wait(barrier, GRP + SLC - 2)

    def req_copy(there, slot):
        return pltpu.make_async_remote_copy(
            src_ref=want.at[there], dst_ref=req_recv.at[slot],
            send_sem=rq_send.at[there], recv_sem=rq_recv.at[slot], device_id={"grp": there},
        )

    def send_req(i, _):
        req_copy(peer(me_g, i, GRP), me_g).start()
        return 0

    lax.fori_loop(0, GRP - 1, send_req, 0)
    req_recv[me_g] = want[me_g]

    def near_copy(there, slot):
        return pltpu.make_async_remote_copy(
            src_ref=near_send.at[there], dst_ref=near_box.at[:, slot],
            send_sem=n_send.at[there], recv_sem=n_recv.at[slot], device_id={"slc": there},
        )

    def send_near(i, _):
        there = peer(me_s, i, SLC)
        for u in range(LIVE):
            near_send[there, u] = slabs[near_idx[LIVE * there + u]]
        near_copy(there, me_s).start()
        return 0

    lax.fori_loop(0, SLC - 1, send_near, 0)
    for u in range(LIVE):
        near_box[u, me_s] = slabs[near_idx[LIVE * me_s + u]]

    def wait_req(i, _):
        there = peer(me_g, i, GRP)
        req_copy(there, there).wait()
        return 0

    lax.fori_loop(0, GRP - 1, wait_req, 0)
    req_local = pltpu.make_async_copy(req_recv, req_smem, loc_sem)
    req_local.start()
    req_local.wait()
    req_out[...] = req_recv[...]

    g_sends, g_recvs, f_sends = (gs0, gs1, gs2), (gr0, gr1, gr2), (fs0, fs1, fs2)

    def grp_copy(c, there, slot):
        return pltpu.make_async_remote_copy(
            src_ref=g_sends[c].at[there], dst_ref=g_recvs[c].at[pl.ds(CAP * slot, CAP)],
            send_sem=g_send.at[c, there], recv_sem=g_recv.at[c, slot], device_id={"grp": there},
        )

    for c, (row, count) in enumerate(CHUNKS):
        rows = pl.ds(row, count)

        def send_grp(i, _, c=c, rows=rows):
            there = peer(me_g, i, GRP)
            for r in range(CAP):
                g_sends[c][there, r] = slabs[req_smem[there, 0, r], rows, :]
            grp_copy(c, there, me_g).start()
            return 0

        lax.fori_loop(0, GRP - 1, send_grp, 0)
        for r in range(CAP):
            g_recvs[c][CAP * me_g + r] = slabs[own_want[r], rows, :]

    def far_copy(c, there, slot):
        row, count = CHUNKS[c]
        return pltpu.make_async_remote_copy(
            src_ref=f_sends[c].at[there], dst_ref=far_box.at[:, slot, pl.ds(row, count)],
            send_sem=f_send.at[c, there], recv_sem=f_recv.at[c, slot], device_id={"slc": there},
        )

    for c, (row, count) in enumerate(CHUNKS):

        def wait_grp(i, _, c=c):
            there = peer(me_g, i, GRP)
            grp_copy(c, there, there).wait_recv()
            return 0

        lax.fori_loop(0, GRP - 1, wait_grp, 0)

        def send_far(i, _, c=c):
            there = peer(me_s, i, SLC)
            for u in range(LIVE):
                f_sends[c][there, u] = g_recvs[c][far_slot[LIVE * there + u]]
            far_copy(c, there, me_s).start()
            return 0

        lax.fori_loop(0, SLC - 1, send_far, 0)
        for u in range(LIVE):
            far_box[u, me_s, row : row + count, :] = g_recvs[c][far_slot[LIVE * me_s + u]]

    def wait_near(i, _):
        there = peer(me_s, i, SLC)
        near_copy(there, there).wait()
        return 0

    lax.fori_loop(0, SLC - 1, wait_near, 0)
    for c in range(len(CHUNKS)):

        def wait_far(i, _, c=c):
            there = peer(me_s, i, SLC)
            far_copy(c, there, there).wait()
            return 0

        lax.fori_loop(0, SLC - 1, wait_far, 0)

        def wait_sent(i, _, c=c):
            there = peer(me_g, i, GRP)
            grp_copy(c, there, there).wait_send()
            return 0

        lax.fori_loop(0, GRP - 1, wait_sent, 0)


def fetch(orb, want, near_idx, far_slot, own_want):
    smem, vmem = pl.BlockSpec(memory_space=pltpu.SMEM), pl.BlockSpec(memory_space=pltpu.VMEM)
    f32 = jnp.float32
    chunk_rows = [count for _, count in CHUNKS]
    n = len(CHUNKS)
    return pl.pallas_call(
        fetch_kernel,
        out_shape=(
            jax.ShapeDtypeStruct((LIVE, SLC, ROWS, LANES), f32),
            jax.ShapeDtypeStruct((LIVE, SLC, ROWS, LANES), f32),
            jax.ShapeDtypeStruct((GRP, 1, LANES), jnp.int32),
        ),
        in_specs=[smem, smem, smem, vmem, vmem],
        out_specs=(vmem, vmem, vmem),
        scratch_shapes=[
            pltpu.VMEM((ORB + 1, ROWS, LANES), f32),
            pltpu.VMEM((SLC, LIVE, ROWS, LANES), f32),
            pltpu.VMEM((GRP, 1, LANES), jnp.int32),
            pltpu.SMEM((GRP, 1, LANES), jnp.int32),
            *[pltpu.VMEM((GRP, CAP, r, LANES), f32) for r in chunk_rows],
            *[pltpu.VMEM((GRP * CAP, r, LANES), f32) for r in chunk_rows],
            *[pltpu.VMEM((SLC, LIVE, r, LANES), f32) for r in chunk_rows],
            pltpu.SemaphoreType.DMA((GRP,)),
            pltpu.SemaphoreType.DMA((GRP,)),
            pltpu.SemaphoreType.DMA((SLC,)),
            pltpu.SemaphoreType.DMA((SLC,)),
            pltpu.SemaphoreType.DMA((n, GRP)),
            pltpu.SemaphoreType.DMA((n, GRP)),
            pltpu.SemaphoreType.DMA((n, SLC)),
            pltpu.SemaphoreType.DMA((n, SLC)),
            pltpu.SemaphoreType.DMA,
        ],
        compiler_params=pltpu.CompilerParams(
            collective_id=0, has_side_effects=True, vmem_limit_bytes=VMEM_LIMIT
        ),
        name="fetch",
    )(near_idx, far_slot, own_want, orb, want)


def answer_kernel(
    pair_of_slot, near_field, far_field,
    near_back, answers,
    fr0, fr1, fr2, gs0, gs1, gs2,
    n_send, n_recv, f_send, f_recv, g_send, g_recv,
):
    me_g = lax.axis_index("grp")
    me_s = lax.axis_index("slc")
    barrier = greet_all(me_g, me_s)
    f_recvs, g_sends = (fr0, fr1, fr2), (gs0, gs1, gs2)
    pl.semaphore_wait(barrier, GRP + SLC - 2)

    def far_copy(c, there, slot):
        row, count = CHUNKS[c]
        return pltpu.make_async_remote_copy(
            src_ref=far_field.at[:, there, pl.ds(row, count)],
            dst_ref=f_recvs[c].at[pl.ds(LIVE * slot, LIVE)],
            send_sem=f_send.at[c, there], recv_sem=f_recv.at[c, slot], device_id={"slc": there},
        )

    for c, (row, count) in enumerate(CHUNKS):

        def send_far(i, _, c=c):
            far_copy(c, peer(me_s, i, SLC), me_s).start()
            return 0

        lax.fori_loop(0, SLC - 1, send_far, 0)
        for u in range(LIVE):
            f_recvs[c][LIVE * me_s + u] = far_field[u, me_s, row : row + count, :]

    def near_copy(there, slot):
        return pltpu.make_async_remote_copy(
            src_ref=near_field.at[:, there], dst_ref=near_back.at[pl.ds(LIVE * slot, LIVE)],
            send_sem=n_send.at[there], recv_sem=n_recv.at[slot], device_id={"slc": there},
        )

    def send_near(i, _):
        near_copy(peer(me_s, i, SLC), me_s).start()
        return 0

    lax.fori_loop(0, SLC - 1, send_near, 0)
    for u in range(LIVE):
        near_back[LIVE * me_s + u] = near_field[u, me_s]

    def grp_copy(c, there, slot):
        row, count = CHUNKS[c]
        return pltpu.make_async_remote_copy(
            src_ref=g_sends[c].at[there], dst_ref=answers.at[slot, :, pl.ds(row, count)],
            send_sem=g_send.at[c, there], recv_sem=g_recv.at[c, slot], device_id={"grp": there},
        )

    for c, (row, count) in enumerate(CHUNKS):

        def wait_far(i, _, c=c):
            there = peer(me_s, i, SLC)
            far_copy(c, there, there).wait_recv()
            return 0

        lax.fori_loop(0, SLC - 1, wait_far, 0)

        def send_grp(i, _, c=c):
            there = peer(me_g, i, GRP)
            for r in range(CAP):
                g_sends[c][there, r] = f_recvs[c][pair_of_slot[CAP * there + r]]
            grp_copy(c, there, me_g).start()
            return 0

        lax.fori_loop(0, GRP - 1, send_grp, 0)
        for r in range(CAP):
            answers[me_g, r, row : row + count, :] = f_recvs[c][pair_of_slot[CAP * me_g + r]]

    def wait_near(i, _):
        there = peer(me_s, i, SLC)
        near_copy(there, there).wait()
        return 0

    lax.fori_loop(0, SLC - 1, wait_near, 0)
    for c in range(len(CHUNKS)):

        def wait_sent(i, _, c=c):
            there = peer(me_s, i, SLC)
            far_copy(c, there, there).wait_send()
            return 0

        lax.fori_loop(0, SLC - 1, wait_sent, 0)

        def wait_grp(i, _, c=c):
            there = peer(me_g, i, GRP)
            grp_copy(c, there, there).wait()
            return 0

        lax.fori_loop(0, GRP - 1, wait_grp, 0)


def answer(near_field, far_field, pair_of_slot):
    smem, vmem = pl.BlockSpec(memory_space=pltpu.SMEM), pl.BlockSpec(memory_space=pltpu.VMEM)
    f32 = jnp.float32
    chunk_rows = [count for _, count in CHUNKS]
    n = len(CHUNKS)
    return pl.pallas_call(
        answer_kernel,
        out_shape=(
            jax.ShapeDtypeStruct((SLC * LIVE, ROWS, LANES), f32),
            jax.ShapeDtypeStruct((GRP, CAP, ROWS, LANES), f32),
        ),
        in_specs=[smem, vmem, vmem],
        out_specs=(vmem, vmem),
        scratch_shapes=[
            *[pltpu.VMEM((SLC * LIVE, r, LANES), f32) for r in chunk_rows],
            *[pltpu.VMEM((GRP, CAP, r, LANES), f32) for r in chunk_rows],
            pltpu.SemaphoreType.DMA((SLC,)),
            pltpu.SemaphoreType.DMA((SLC,)),
            pltpu.SemaphoreType.DMA((n, SLC)),
            pltpu.SemaphoreType.DMA((n, SLC)),
            pltpu.SemaphoreType.DMA((n, GRP)),
            pltpu.SemaphoreType.DMA((n, GRP)),
        ],
        compiler_params=pltpu.CompilerParams(
            collective_id=1, has_side_effects=True, vmem_limit_bytes=VMEM_LIMIT
        ),
        name="answer",
    )(pair_of_slot, near_field, far_field)


def split(values):
    high = values.astype(jnp.bfloat16)
    return high, (values - high.astype(jnp.float32)).astype(jnp.bfloat16)


def dot(left, right, dims=((1,), (0,))):
    return lax.dot_general(left, right, (dims, ((), ())), preferred_element_type=jnp.float32)


def plane_at(shape, dim):
    row = lax.broadcasted_iota(jnp.int32, shape, dim)
    return 3 * lax.rem(row, SLC) + lax.div(row, SLC)


def pair_kernel(
    gaps, near_box, far_box, qc_high, qc_low, qa_high, qa_low, q_b, lam_b, lam_ac,
    near_field, far_field,
    psi, moved, box, modes,
):
    lane = lax.broadcasted_iota(jnp.int32, (8, CELLS), 1)[:1]
    at_b, at_c = lax.div(lane, B), lax.rem(lane, B)
    place, shift_mat = [], []
    for u in range(LIVE):
        e0, e1, e2 = gaps[3 * u], gaps[3 * u + 1], gaps[3 * u + 2]
        turn = e1 * B + e2
        place.append(turn)
        inside = (at_b + e1 >= 0) & (at_b + e1 < B) & (at_c + e2 >= 0) & (at_c + e2 < B)
        inside = jnp.where(inside, 1.0, 0.0).astype(jnp.float32)
        wanted, held = plane_at((B, B), 0) + e0, plane_at((B, B), 1)
        onehot = jnp.where(wanted == held, 1.0, 0.0).astype(jnp.bfloat16)
        shift_mat.append((onehot, inside))
        for q in range(BLOCKS):
            cols = slice(q * LANES, (q + 1) * LANES)
            for p in range(PLANES):
                rows = slice(u * B + p * SLC, u * B + (p + 1) * SLC)
                where = pl.ds(3 * q + p, SLC, stride=ROWS)
                psi[rows, cols] = near_box[u, where, :]
                box[rows, cols] = far_box[u, where, :]
        mine = slice(u * B, (u + 1) * B)
        back = jnp.where(turn > 0, CELLS - turn, -turn)
        turned = pltpu.roll(box[mine, :], back, 1) * inside
        high, low = split(turned)
        moved[mine, :] = dot(onehot, high) + dot(onehot, low)

    for g in range(CELLS // WIDE):
        cols = slice(g * WIDE, (g + 1) * WIDE)
        high, low = split(psi[:, cols] * moved[:, cols])
        part = dot(high, qc_high[...]) + dot(low, qc_high[...]) + dot(high, qc_low[...])
        high, low = split(part)
        over = ((0,), (0,))
        modes[cols, :] = (
            dot(high, qa_high[...], over) + dot(low, qa_high[...], over) + dot(high, qa_low[...], over)
        )

    def along_b(values):
        high, low = split(values)
        return dot(q_b[...], jnp.concatenate([high, high, low], axis=0))

    def weigh(i, _):
        even, odd = pl.ds(2 * i, B, stride=B), pl.ds(2 * i + 1, B, stride=B)
        values = along_b(jnp.concatenate([modes[even, :], modes[odd, :]], axis=1))
        total = jnp.concatenate([lam_b[...], lam_b[...]], axis=1) + lam_ac[i]
        values = along_b(values / total)
        modes[even, :] = values[:, :LANES]
        modes[odd, :] = values[:, LANES:]
        return 0

    lax.fori_loop(0, B // 2, weigh, 0, unroll=2)

    for g in range(CELLS // WIDE):
        cols = slice(g * WIDE, (g + 1) * WIDE)
        high, low = split(modes[cols, :])
        over = ((1,), (1,))
        part = (
            dot(qa_high[...], high, over) + dot(qa_high[...], low, over) + dot(qa_low[...], high, over)
        )
        high, low = split(part)
        box[:, cols] = dot(high, qc_high[...]) + dot(low, qc_high[...]) + dot(high, qc_low[...])

    for u in range(LIVE):
        mine = slice(u * B, (u + 1) * B)
        onehot, inside = shift_mat[u]
        potential = box[mine, :]
        moved[mine, :] = potential * moved[mine, :]
        high, low = split(potential * psi[mine, :] * inside)
        over = ((0,), (0,))
        forth = jnp.where(place[u] < 0, place[u] + CELLS, place[u])
        box[mine, :] = pltpu.roll(dot(onehot, high, over) + dot(onehot, low, over), forth, 1)
        for q in range(BLOCKS):
            cols = slice(q * LANES, (q + 1) * LANES)
            for p in range(PLANES):
                rows = slice(u * B + p * SLC, u * B + (p + 1) * SLC)
                where = pl.ds(3 * q + p, SLC, stride=ROWS)
                near_field[u, where, :] = moved[rows, cols]
                far_field[u, where, :] = box[rows, cols]
        for extra in (54, 55):
            where = pl.ds(extra, SLC, stride=ROWS)
            near_field[u, where, :] = jnp.zeros((SLC, LANES), jnp.float32)
            far_field[u, where, :] = jnp.zeros((SLC, LANES), jnp.float32)


def pairs(gaps, near_box, far_box):
    smem, vmem = pl.BlockSpec(memory_space=pltpu.SMEM), pl.BlockSpec(memory_space=pltpu.VMEM)
    flat = (LIVE, SLC * ROWS, LANES)
    constants = [jnp.asarray(t) for t in tables()]
    near, far = pl.pallas_call(
        pair_kernel,
        out_shape=(jax.ShapeDtypeStruct(flat, jnp.float32),) * 2,
        in_specs=[smem] + [vmem] * (2 + len(constants)),
        out_specs=(vmem, vmem),
        scratch_shapes=[
            pltpu.VMEM((LIVE * B, CELLS), jnp.float32),
            pltpu.VMEM((LIVE * B, CELLS), jnp.float32),
            pltpu.VMEM((LIVE * B, CELLS), jnp.float32),
            pltpu.VMEM((CELLS, LANES), jnp.float32),
        ],
        compiler_params=pltpu.CompilerParams(vmem_limit_bytes=VMEM_LIMIT),
        name="pairs",
    )(gaps, near_box.reshape(flat), far_box.reshape(flat), *constants)
    shape = (LIVE, SLC, ROWS, LANES)
    return near.reshape(shape), far.reshape(shape)


def sum_kernel(near_idx, requested, orb, pot, near_back, answers, out, total):
    total[...] = jnp.zeros_like(total)

    def add_near(t, _):
        total[near_idx[t]] += near_back[t]
        return 0

    def add_far(t, _):
        total[requested[t]] += answers[t]
        return 0

    lax.fori_loop(0, SLC * LIVE, add_near, 0)
    lax.fori_loop(0, GRP * CAP, add_far, 0)
    for q in range(BLOCKS):
        cols = slice(q * LANES, (q + 1) * LANES)
        out[:, :, cols] = pot[:, :, cols] * orb[:, :, cols] - total[:ORB, 3 * q : 3 * q + 3, :]


def sums(orb, pot, near_back, answers, near_idx, requested):
    smem, vmem = pl.BlockSpec(memory_space=pltpu.SMEM), pl.BlockSpec(memory_space=pltpu.VMEM)
    return pl.pallas_call(
        sum_kernel,
        out_shape=jax.ShapeDtypeStruct(orb.shape, jnp.float32),
        in_specs=[smem, smem, vmem, vmem, vmem, vmem],
        out_specs=vmem,
        scratch_shapes=[pltpu.VMEM((ORB + 1, ROWS, LANES), jnp.float32)],
        compiler_params=pltpu.CompilerParams(vmem_limit_bytes=VMEM_LIMIT),
        name="sums",
    )(near_idx, requested, orb, pot, near_back, answers.reshape(GRP * CAP, ROWS, LANES))


def pick(values, index, count):
    hot = index[:, None] == jnp.arange(count, dtype=jnp.int32)[None, :]
    return jnp.sum(jnp.where(hot, values[None, :], 0), axis=1)


def per_device(orbitals, local_pot, pair_owner, pair_remote, pair_resident, pair_count, offsets):
    me_g = lax.axis_index("grp")
    me_s = lax.axis_index("slc")
    owner, remote, resident, count = pair_owner[0, :, 0], pair_remote[0], pair_resident[0], pair_count[0]
    t = jnp.arange(SLC * LIVE, dtype=jnp.int32)
    earlier = (t[None, :] < t[:, None]) & (owner[None, :] == owner[:, None])
    slot = owner * CAP + jnp.sum(earlier.astype(jnp.int32), axis=1)
    place = jnp.arange(GRP * CAP, dtype=jnp.int32)
    named = slot[None, :] == place[:, None]
    used = jnp.any(named, axis=1)
    want = jnp.where(used, jnp.sum(jnp.where(named, remote[None, :], 0), axis=1), ORB)
    pair_of_slot = jnp.sum(jnp.where(named, t[None, :], 0), axis=1)
    u = jnp.arange(SLC, dtype=jnp.int32)
    running = jnp.sum(jnp.where(u[None, :] <= u[:, None], count[None, :], 0), axis=1)
    home = jnp.sum((running[None, :] <= t[:, None]).astype(jnp.int32), axis=1)
    near_idx = home * 2 + resident
    near_orb, far_orb = me_g * ORB + near_idx, owner * ORB + remote
    own = lax.dynamic_slice_in_dim(jnp.stack([near_orb, far_orb], axis=1), me_s * LIVE, LIVE)
    gaps = (jnp.take(offsets, own[:, 0], axis=0) - jnp.take(offsets, own[:, 1], axis=0)).reshape(-1)

    want_rows = jnp.pad(want.reshape(GRP, 1, CAP), ((0, 0), (0, 0), (0, LANES - CAP)))
    own_want = lax.dynamic_slice_in_dim(want, me_g * CAP, CAP)
    near_box, far_box, req = fetch(orbitals, want_rows, near_idx, slot, own_want)
    requested = req[:, 0, :CAP].reshape(-1)
    near_field, far_field = pairs(gaps, near_box, far_box)
    near_back, answers = answer(near_field, far_field, pair_of_slot)
    return sums(orbitals, local_pot, near_back, answers, near_idx, requested)


def solution(mesh):
    in_specs = (
        P("grp", "slc", None),
        P("grp", "slc", None),
        P("grp", None, None),
        P("grp", None),
        P("grp", None),
        P("grp", None),
        P(),
    )
    return jax.shard_map(
        per_device, mesh=mesh, in_specs=in_specs, out_specs=P("grp", "slc", None), check_vma=False
    )
```

```python
import functools

import jax
import jax.numpy as jnp
import numpy as np
from jax import lax
from jax.experimental import pallas as pl
from jax.experimental.pallas import tpu as pltpu
from jax.sharding import PartitionSpec as P

B = 48
CELLS = B * B
LANES = 128
BLOCKS = CELLS // LANES
PLANES = 3
ROWS = 56
GRP = 32
SLC = 16
ORB = 32
PAIRS = 32
HALVES = 2
CHUNKS = ((0, 32), (32, 24))
MARGIN = 9
WIDE = 384
VMEM_LIMIT = 60 * 1024 * 1024

NEAR, OWNER, FAR, SEAT, WANT = 0, 1, 2, 3, 5
GAP, BLOCK, REST = 8, 11, 13


def split_np(values):
    high = values.astype(jnp.bfloat16)
    low = (values - high.astype(np.float64)).astype(jnp.bfloat16)
    return high, low


@functools.cache
def tables():
    k = np.arange(B, dtype=np.float64)
    q = np.sqrt(2.0 / (B + 1)) * np.sin(np.pi * np.outer(k + 1, k + 1) / (B + 1))
    lam = 2.0 - 2.0 * np.cos(np.pi * (k + 1) / (B + 1))
    plane_of = 3 * (np.arange(B) % SLC) + np.arange(B) // SLC
    q_c = np.kron(np.eye(WIDE // B), q)
    q_a = np.zeros((B, LANES))
    q_a[:, :B] = q[plane_of]
    q_high, q_low = split_np(q)
    q_b = np.concatenate([q_high, q_low, q_high], axis=1)
    lam_b = np.broadcast_to(lam[:, None], (B, 2 * LANES)).astype(np.float32)
    lane = np.arange(LANES)
    lam_a = np.where(lane < B, lam[lane % B], 1.0)
    lam_ac = np.zeros((B // 2, 1, 2 * LANES), np.float32)
    for kc in range(B):
        lam_ac[kc // 2, 0, (kc % 2) * LANES : (kc % 2 + 1) * LANES] = lam_a + lam[kc]
    return (*split_np(q_c), *split_np(q_a), q_b, lam_b, lam_ac)


def iota(shape, dim):
    return lax.broadcasted_iota(jnp.int32, shape, dim)


def total_of(mask, values, axis):
    return jnp.sum(jnp.where(mask, values, 0), axis=axis, keepdims=True)


def index_tables(owner, remote, resident, count):
    square = (PAIRS, PAIRS)
    down, across = iota(square, 0), iota(square, 1)

    def as_column(row):
        return total_of(down == across, row, 1)

    owner_col = as_column(owner)
    same = owner_col == owner
    ones = jnp.ones(square, jnp.int32)

    def places(before, axis, other_axis):
        return total_of(same & before, ones, axis), total_of(same, ones, axis)

    rank_row, times_row = places(down < across, 0, 1)
    rank_col, times_col = places(across < down, 1, 0)

    def seats(rank, times, rank_other, times_other, before, axis):
        single, first, second = times == 1, (times == 2) & (rank == 0), rank == 1
        single_o, first_o, second_o = times_other == 1, (times_other == 2) & (rank_other == 0), rank_other == 1
        twice = jnp.sum(jnp.where(second_o, 1, 0), axis=axis, keepdims=True)
        at_first = total_of(before & first_o, ones, axis)
        at_second = total_of(before & second_o, ones, axis)
        filled = twice + total_of(before & single_o, ones, axis)
        late = single & (filled >= SLC)
        half = jnp.where(second | late, 1, 0)
        seat = jnp.where(
            first, at_first, jnp.where(second, at_second, jnp.where(late, filled - SLC + twice, filled))
        )
        return half, seat

    half_row, seat_row = seats(rank_row, times_row, rank_col, times_col, down < across, 0)
    half_col, seat_col = seats(rank_col, times_col, rank_row, times_row, across < down, 1)

    upto = iota((SLC, SLC), 1) <= iota((SLC, SLC), 0)
    running = total_of(upto, count, 1)
    home = jnp.sum(jnp.where(running <= iota((SLC, PAIRS), 1), 1, 0), axis=0, keepdims=True)
    near_col = as_column(home * 2 + resident)
    remote_col = as_column(remote)

    wide = (PAIRS, LANES)
    lane = iota(wide, 1)
    seated = (half_col * SLC + seat_col) == lane
    rows = [jnp.zeros((1, LANES), jnp.int32)] * 8
    rows[NEAR] = total_of(seated, near_col + jnp.zeros(wide, jnp.int32), 0)
    rows[OWNER] = total_of(seated, owner_col + jnp.zeros(wide, jnp.int32), 0)
    rows[FAR] = total_of(seated, owner_col * ORB + remote_col + jnp.zeros(wide, jnp.int32), 0)
    requests = jnp.zeros((GRP, LANES), jnp.int32)
    for h in range(HALVES):
        named = (owner_col == lane) & (half_col == h)
        rows[SEAT + h] = total_of(named, seat_col + jnp.zeros(wide, jnp.int32), 0)
        rows[WANT + h] = ORB + total_of(named, remote_col - ORB + jnp.zeros(wide, jnp.int32), 0)
        asked = (down == owner) & (half_row == h)
        want_col = ORB + total_of(asked, remote - ORB + jnp.zeros(square, jnp.int32), 1)
        requests = jnp.where(iota((GRP, LANES), 1) == h, want_col, requests)
    for n, most in ((NEAR, ORB - 1), (OWNER, GRP - 1), (SEAT, SLC - 1), (SEAT + 1, SLC - 1), (WANT, ORB), (WANT + 1, ORB)):
        rows[n] = jnp.clip(rows[n], 0, most)
    return rows, jnp.clip(requests, 0, ORB)


def shift_rows(rows, offsets, me_g, me_s):
    lane = iota((1, LANES), 1)
    orbital = iota(offsets.shape, 1)
    rows += [jnp.zeros((1, LANES), jnp.int32) for _ in range(8)]
    for h in range(HALVES):
        mine = lane == SLC * h + me_s
        near = me_g * ORB + total_of(mine, rows[NEAR], 1)
        far = total_of(mine, rows[FAR], 1)
        gap = total_of(orbital == near, offsets, 1) - total_of(orbital == far, offsets, 1)
        for k in range(3):
            rows[GAP + k] = jnp.where(lane == h, gap[k : k + 1], rows[GAP + k])
        turn = gap[1:2] * B + gap[2:3]
        for n, sign in enumerate((1, -1)):
            reach = sign * turn + MARGIN * LANES
            reach = jnp.clip(reach, 0, (2 * MARGIN) * LANES - 1)
            block = lax.div(reach, jnp.full_like(reach, LANES))
            rows[BLOCK + n] = jnp.where(lane == h, block, rows[BLOCK + n])
            rows[REST + n] = jnp.where(lane == h, reach - block * LANES, rows[REST + n])


def stack_rows(rows):
    at = iota((len(rows), LANES), 0)
    table = jnp.zeros((len(rows), LANES), jnp.int32)
    for n, row in enumerate(rows):
        table = jnp.where(at == n, row, table)
    return table


def split(values):
    high = values.astype(jnp.bfloat16)
    return high, (values - high.astype(jnp.float32)).astype(jnp.bfloat16)


def dot(left, right, dims=((1,), (0,))):
    return lax.dot_general(left, right, (dims, ((), ())), preferred_element_type=jnp.float32)


def plane_at(shape, dim):
    row = iota(shape, dim)
    return 3 * lax.rem(row, SLC) + lax.div(row, SLC)


GROUPS = [slice(g * WIDE, (g + 1) * WIDE) for g in range(CELLS // WIDE)]


def wire_places():
    for q in range(BLOCKS):
        for p in range(PLANES):
            yield (
                pl.ds(3 * q + p, SLC, stride=ROWS),
                slice(p * SLC, (p + 1) * SLC),
                slice(q * LANES, (q + 1) * LANES),
            )


def lane_shift(blocks, block, rest):
    loaded = [blocks[block + q] for q in range(BLOCKS + 1)]
    near, over = jnp.concatenate(loaded[:-1], axis=0), jnp.concatenate(loaded[1:], axis=0)
    high, low = split(jnp.concatenate([near, over], axis=1))
    square = (2 * LANES, LANES)
    onehot = jnp.where(iota(square, 0) == iota(square, 1) + rest, 1.0, 0.0).astype(jnp.bfloat16)
    out = dot(high, onehot) + dot(low, onehot)
    return jnp.concatenate([out[q * B : (q + 1) * B] for q in range(BLOCKS)], axis=1)


def pair_fields(gap, there, back, near_box, far_box, near_field, far_field, consts, scratch):
    qc_high, qc_low, qa_high, qa_low, q_b, lam_b, lam_ac = consts
    psi, moved, blocks, modes = scratch
    e0, e1, e2 = gap
    lane = iota((8, CELLS), 1)[:1]
    at_b, at_c = lax.div(lane, B) + e1, lax.rem(lane, B) + e2
    inside = (at_b >= 0) & (at_b < B) & (at_c >= 0) & (at_c < B)
    inside = jnp.where(inside, 1.0, 0.0).astype(jnp.float32)
    onehot = jnp.where(plane_at((B, B), 0) + e0 == plane_at((B, B), 1), 1.0, 0.0).astype(jnp.bfloat16)
    for where, rows, cols in wire_places():
        psi[rows, cols] = near_box[where, :]
        blocks[MARGIN + cols.start // LANES, rows, :] = far_box[where, :]
    high, low = split(lane_shift(blocks, *there) * inside)
    moved[...] = dot(onehot, high) + dot(onehot, low)

    density = jnp.concatenate([psi[:, cols] * moved[:, cols] for cols in GROUPS], axis=0)
    high, low = split(density)
    part = dot(high, qc_high[...]) + dot(low, qc_high[...]) + dot(high, qc_low[...])
    for g, cols in enumerate(GROUPS):
        high, low = split(part[g * B : (g + 1) * B])
        over = ((0,), (0,))
        modes[cols, :] = (
            dot(high, qa_high[...], over) + dot(low, qa_high[...], over) + dot(high, qa_low[...], over)
        )

    def along_b(values):
        high, low = split(values)
        return dot(q_b[...], jnp.concatenate([high, high, low], axis=0))

    def weigh(i, _):
        even, odd = pl.ds(2 * i, B, stride=B), pl.ds(2 * i + 1, B, stride=B)
        values = along_b(jnp.concatenate([modes[even, :], modes[odd, :]], axis=1))
        values = along_b(values / (lam_b[...] + lam_ac[i]))
        modes[even, :] = values[:, :LANES]
        modes[odd, :] = values[:, LANES:]
        return 0

    lax.fori_loop(0, B // 2, weigh, 0, unroll=2)

    parts = []
    for cols in GROUPS:
        high, low = split(modes[cols, :])
        over = ((1,), (1,))
        parts.append(
            dot(qa_high[...], high, over) + dot(qa_high[...], low, over) + dot(qa_low[...], high, over)
        )
    high, low = split(jnp.concatenate(parts, axis=0))
    potential = dot(high, qc_high[...]) + dot(low, qc_high[...]) + dot(high, qc_low[...])
    for g, cols in enumerate(GROUPS):
        here = potential[g * B : (g + 1) * B]
        moved[:, cols] = here * moved[:, cols]
        high, low = split(here * psi[:, cols] * inside[:, cols])
        over = ((0,), (0,))
        apart = dot(onehot, high, over) + dot(onehot, low, over)
        for n in range(WIDE // LANES):
            blocks[MARGIN + cols.start // LANES + n] = apart[:, n * LANES : (n + 1) * LANES]
    far = lane_shift(blocks, *back)
    for where, rows, cols in wire_places():
        near_field[where, :] = moved[rows, cols]
        far_field[where, :] = far[rows, cols]


def peer(me, i, count):
    return lax.rem(me + (i // 2 + 1) * (1 - 2 * (i % 2)) + count, count)


def part_of(slot, count):
    return pl.ds(pl.multiple_of(slot * count, 8), count)


def rows_of(slot, row, count):
    return pl.ds(pl.multiple_of(slot * ROWS + row, 8), count)


N = len(CHUNKS)


def exchange_kernel(*refs):
    names = iter(refs)

    def take(count=1):
        out = [next(names) for _ in range(count)]
        return out[0] if count == 1 else out

    def halves():
        return take(HALVES)

    def chunked():
        return [take(N) for _ in range(HALVES)]

    owner, remote, resident, count_row, offsets, orb_hbm = take(6)
    consts_hbm = take(7)
    near_back, answers = halves(), halves()
    table_out, req_recv = take(2)
    orb, slabs, want, table_smem, req_smem = take(5)
    consts = take(7)
    near_send, near_box, far_box, near_field, far_field = (halves() for _ in range(5))
    g_send, g_recv, f_send, f_back, a_send = (chunked() for _ in range(5))
    scratch = take(4)
    local_sem, const_sem, rq_s, rq_r, near_s, near_r, nback_s, nback_r = take(8)
    grp_s, grp_r, far_s, far_r, fback_s, fback_r, ans_s, ans_r = take(8)

    me_g, me_s = lax.axis_index("grp"), lax.axis_index("slc")

    def each(axis, action):
        me, count = (me_g, GRP) if axis == "grp" else (me_s, SLC)

        def step(i, _):
            action(peer(me, i, count))
            return 0

        lax.fori_loop(0, count - 1, step, 0)

    orb_copy = pltpu.make_async_copy(orb_hbm, orb, local_sem.at[2])
    orb_copy.start()
    const_copies = [pltpu.make_async_copy(a, b, const_sem.at[n]) for n, (a, b) in enumerate(zip(consts_hbm, consts))]
    for copy in const_copies:
        copy.start()
    barrier = pltpu.get_barrier_semaphore()
    each("grp", lambda there: pl.semaphore_signal(barrier, inc=1, device_id={"grp": there}))
    each("slc", lambda there: pl.semaphore_signal(barrier, inc=1, device_id={"slc": there}))

    rows, requests = index_tables(owner[...], remote[...], resident[...], count_row[...])
    shift_rows(rows, offsets[...], me_g, me_s)
    table_out[...] = stack_rows(rows)
    want[...] = requests.reshape(GRP, 1, LANES)
    local = pltpu.make_async_copy(table_out, table_smem, local_sem.at[0])
    local.start()
    orb_copy.wait()
    for q in range(BLOCKS):
        for p in range(PLANES):
            slabs[:ORB, 3 * q + p, :] = orb[p, :, q * LANES : (q + 1) * LANES]
    slabs[:ORB, 54:56, :] = jnp.zeros((ORB, 2, LANES), jnp.float32)
    slabs[ORB] = jnp.zeros((ROWS, LANES), jnp.float32)
    blocks = scratch[2]
    blocks[...] = jnp.zeros_like(blocks)
    local.wait()
    pl.semaphore_wait(barrier, GRP + SLC - 2)

    def remote_copy(src, dst, send, recv, axis, there):
        return pltpu.make_async_remote_copy(
            src_ref=src, dst_ref=dst, send_sem=send, recv_sem=recv, device_id={axis: there}
        )

    def req_copy(there, slot):
        return remote_copy(want.at[there], req_recv.at[slot], rq_s.at[0], rq_r.at[0], "grp", there)

    def near_copy(h, there, slot):
        return remote_copy(
            near_send[h].at[part_of(there, ROWS)], near_box[h].at[part_of(slot, ROWS)],
            near_s.at[h], near_r.at[h], "slc", there,
        )

    def grp_copy(h, c, there, slot):
        return remote_copy(
            g_send[h][c].at[there], g_recv[h][c].at[slot], grp_s.at[N * h + c], grp_r.at[N * h + c], "grp", there
        )

    def far_copy(h, c, there, slot):
        row, count = CHUNKS[c]
        return remote_copy(
            f_send[h][c].at[there], far_box[h].at[rows_of(slot, row, count)],
            far_s.at[N * h + c], far_r.at[N * h + c], "slc", there,
        )

    def fback_copy(h, c, there, slot):
        row, count = CHUNKS[c]
        return remote_copy(
            far_field[h].at[rows_of(there, row, count)], f_back[h][c].at[slot],
            fback_s.at[N * h + c], fback_r.at[N * h + c], "slc", there,
        )

    def nback_copy(h, there, slot):
        return remote_copy(
            near_field[h].at[part_of(there, ROWS)], near_back[h].at[part_of(slot, ROWS)],
            nback_s.at[h], nback_r.at[h], "slc", there,
        )

    def ans_copy(h, c, there, slot):
        row, count = CHUNKS[c]
        return remote_copy(
            a_send[h][c].at[there], answers[h].at[rows_of(slot, row, count)],
            ans_s.at[N * h + c], ans_r.at[N * h + c], "grp", there,
        )

    def all_of(ref, size, send, recv, axis):
        me, count = (me_g, GRP) if axis == "grp" else (me_s, SLC)
        whole = ref.at[pl.ds(0, size)]
        return remote_copy(whole, whole, send, recv, axis, peer(me, 0, count))

    def all_req():
        return all_of(req_recv, GRP - 1, rq_s.at[0], rq_r.at[0], "grp")

    def all_near(h):
        return all_of(near_box[h], (SLC - 1) * ROWS, near_s.at[h], near_r.at[h], "slc")

    def all_grp(h, c):
        return all_of(g_recv[h][c], GRP - 1, grp_s.at[N * h + c], grp_r.at[N * h + c], "grp")

    def all_far(h, c):
        return all_of(f_send[h][c], SLC - 1, far_s.at[N * h + c], far_r.at[N * h + c], "slc")

    def all_fback(h, c):
        return all_of(f_back[h][c], SLC - 1, fback_s.at[N * h + c], fback_r.at[N * h + c], "slc")

    def all_nback(h):
        return all_of(near_back[h], (SLC - 1) * ROWS, nback_s.at[h], nback_r.at[h], "slc")

    def all_ans(h, c):
        return all_of(a_send[h][c], GRP - 1, ans_s.at[N * h + c], ans_r.at[N * h + c], "grp")

    def send_near(h):
        def one(there):
            near_send[h][part_of(there, ROWS), :] = slabs[table_smem[NEAR, SLC * h + there]]
            near_copy(h, there, me_s).start()

        each("slc", one)
        near_box[h][part_of(me_s, ROWS), :] = slabs[table_smem[NEAR, SLC * h + me_s]]

    def send_grp(h, c):
        row, count = CHUNKS[c]

        def one(there):
            g_send[h][c][there] = slabs[req_smem[there, 0, h], row : row + count, :]
            grp_copy(h, c, there, me_g).start()

        each("grp", one)
        g_recv[h][c][me_g] = slabs[table_smem[WANT + h, me_g], row : row + count, :]

    def forward_far(h, c):
        row, count = CHUNKS[c]
        all_grp(h, c).wait_recv()

        def one(there):
            f_send[h][c][there] = g_recv[h][c][table_smem[OWNER, SLC * h + there]]
            far_copy(h, c, there, me_s).start()

        each("slc", one)
        far_box[h][rows_of(me_s, row, count), :] = g_recv[h][c][table_smem[OWNER, SLC * h + me_s]]

    def compute(h):
        all_near(h).wait_recv()
        for c in range(N):
            all_far(h, c).wait_recv()
        gap = [table_smem[GAP + k, h] for k in range(3)]
        there, back = [(table_smem[BLOCK + n, h], table_smem[REST + n, h]) for n in range(2)]
        pair_fields(gap, there, back, near_box[h], far_box[h], near_field[h], far_field[h], consts, scratch)

    def send_fields(h):
        for c, (row, count) in enumerate(CHUNKS):
            each("slc", lambda there: fback_copy(h, c, there, me_s).start())
            f_back[h][c][me_s] = far_field[h][rows_of(me_s, row, count), :]

    def send_near_fields(h):
        each("slc", lambda there: nback_copy(h, there, me_s).start())
        near_back[h][part_of(me_s, ROWS), :] = near_field[h][part_of(me_s, ROWS), :]

    def send_answers(h, c):
        row, count = CHUNKS[c]
        all_fback(h, c).wait_recv()

        def one(there):
            a_send[h][c][there] = f_back[h][c][table_smem[SEAT + h, there]]
            ans_copy(h, c, there, me_g).start()

        each("grp", one)
        answers[h][rows_of(me_g, row, count), :] = f_back[h][c][table_smem[SEAT + h, me_g]]

    each("grp", lambda there: req_copy(there, me_g).start())
    req_recv[me_g] = want[me_g]
    send_near(0)
    all_req().wait_recv()
    asked = pltpu.make_async_copy(req_recv, req_smem, local_sem.at[1])
    asked.start()
    asked.wait()
    for c in range(N):
        send_grp(0, c)
    for c in range(N):
        forward_far(0, c)
        send_grp(1, c)
    send_near(1)
    for copy in const_copies:
        copy.wait()
    compute(0)
    send_fields(0)
    for c in range(N):
        forward_far(1, c)
        send_answers(0, c)
    send_near_fields(0)
    compute(1)
    send_fields(1)
    for c in range(N):
        send_answers(1, c)
    send_near_fields(1)

    all_req().wait_send()
    for h in range(HALVES):
        all_near(h).wait_send()
        all_nback(h).wait()
        for c in range(N):
            all_grp(h, c).wait_send()
            all_far(h, c).wait_send()
            all_fback(h, c).wait_send()
            all_ans(h, c).wait()


def exchange(owner, remote, resident, count, offsets, orb):
    vmem = pl.BlockSpec(memory_space=pltpu.VMEM)

    def slots(number):
        return pltpu.VMEM((number * ROWS, LANES), jnp.float32)

    def out(number):
        return jax.ShapeDtypeStruct((number * ROWS, LANES), jnp.float32)

    def chunked(number):
        return [pltpu.VMEM((number, rows, LANES), jnp.float32) for _ in range(HALVES) for _, rows in CHUNKS]

    hbm = pl.BlockSpec(memory_space=pltpu.HBM)
    consts = [jnp.asarray(t) for t in tables()]

    def sems(number):
        return [pltpu.SemaphoreType.DMA((number,))] * 2

    return pl.pallas_call(
        exchange_kernel,
        out_shape=[
            *[out(SLC)] * HALVES,
            *[out(GRP)] * HALVES,
            jax.ShapeDtypeStruct((16, LANES), jnp.int32),
            jax.ShapeDtypeStruct((GRP, 1, LANES), jnp.int32),
        ],
        in_specs=[vmem, vmem, vmem, vmem, vmem, hbm, *[hbm] * len(consts)],
        out_specs=[vmem] * 6,
        scratch_shapes=[
            pltpu.VMEM(orb.shape, jnp.float32),
            pltpu.VMEM((ORB + 1, ROWS, LANES), jnp.float32),
            pltpu.VMEM((GRP, 1, LANES), jnp.int32),
            pltpu.SMEM((16, LANES), jnp.int32),
            pltpu.SMEM((GRP, 1, LANES), jnp.int32),
            *[pltpu.VMEM(t.shape, t.dtype) for t in consts],
            *[slots(SLC)] * (5 * HALVES),
            *chunked(GRP),
            *chunked(GRP),
            *chunked(SLC),
            *chunked(SLC),
            *chunked(GRP),
            *[pltpu.VMEM((B, CELLS), jnp.float32)] * 2,
            pltpu.VMEM((2 * MARGIN + BLOCKS, B, LANES), jnp.float32),
            pltpu.VMEM((CELLS, LANES), jnp.float32),
            pltpu.SemaphoreType.DMA((3,)),
            pltpu.SemaphoreType.DMA((len(consts),)),
            *sems(1),
            *sems(HALVES),
            *sems(HALVES),
            *sems(HALVES * N),
            *sems(HALVES * N),
            *sems(HALVES * N),
            *sems(HALVES * N),
        ],
        compiler_params=pltpu.CompilerParams(
            collective_id=0, has_side_effects=True, vmem_limit_bytes=VMEM_LIMIT
        ),
        name="exchange",
    )(owner, remote, resident, count, offsets, orb, *consts)


def sum_kernel(table, requested, orb_hbm, pot_hbm, near_0, near_1, answers_0, answers_1, out, total, orb, pot, sem):
    copies = [
        pltpu.make_async_copy(orb_hbm, orb, sem.at[0]),
        pltpu.make_async_copy(pot_hbm, pot, sem.at[1]),
    ]
    for copy in copies:
        copy.start()
    total[...] = jnp.zeros_like(total)

    def add(source, t, place):
        total[part_of(place, ROWS), :] += source[part_of(t, ROWS), :]

    def add_near(t, _):
        add(near_0, t, table[NEAR, t])
        add(near_1, t, table[NEAR, SLC + t])
        return 0

    def add_far(t, _):
        add(answers_0, t, requested[t, 0, 0])
        add(answers_1, t, requested[t, 0, 1])
        return 0

    lax.fori_loop(0, SLC, add_near, 0)
    lax.fori_loop(0, GRP, add_far, 0)
    for copy in copies:
        copy.wait()
    for q in range(BLOCKS):
        for p in range(PLANES):
            cols = slice(q * LANES, (q + 1) * LANES)
            field = total[pl.ds(3 * q + p, ORB, stride=ROWS), :]
            out[p, :, cols] = pot[p, :, cols] * orb[p, :, cols] - field


def sums(table, requested, orb, pot, fields):
    smem, vmem = pl.BlockSpec(memory_space=pltpu.SMEM), pl.BlockSpec(memory_space=pltpu.VMEM)
    return pl.pallas_call(
        sum_kernel,
        out_shape=jax.ShapeDtypeStruct(orb.shape, jnp.float32),
        in_specs=[smem, smem, *[pl.BlockSpec(memory_space=pltpu.HBM)] * 2, *[vmem] * 4],
        out_specs=vmem,
        scratch_shapes=[
            pltpu.VMEM(((ORB + 1) * ROWS, LANES), jnp.float32),
            *[pltpu.VMEM(orb.shape, jnp.float32)] * 2,
            pltpu.SemaphoreType.DMA((2,)),
        ],
        compiler_params=pltpu.CompilerParams(vmem_limit_bytes=VMEM_LIMIT),
        name="sums",
    )(table, requested, orb, pot, *fields)


def per_device(orbitals, local_pot, pair_owner, pair_remote, pair_resident, pair_count, offsets):
    orb, pot = jnp.transpose(orbitals, (1, 0, 2)), jnp.transpose(local_pot, (1, 0, 2))
    *fields, table, requested = exchange(
        pair_owner.reshape(1, PAIRS), pair_remote, pair_resident, pair_count, offsets.T, orb
    )
    return jnp.transpose(sums(table, requested, orb, pot, fields), (1, 0, 2))


def solution(mesh):
    in_specs = (
        P("grp", "slc", None),
        P("grp", "slc", None),
        P("grp", None, None),
        P("grp", None),
        P("grp", None),
        P("grp", None),
        P(),
    )
    return jax.shard_map(
        per_device, mesh=mesh, in_specs=in_specs, out_specs=P("grp", "slc", None), check_vma=False
    )
```

```python
import functools

import jax
import jax.numpy as jnp
import numpy as np
from jax import lax
from jax.experimental import pallas as pl
from jax.experimental.pallas import tpu as pltpu
from jax.sharding import PartitionSpec as P

B = 48
CELLS = B * B
LANES = 128
BLOCKS = CELLS // LANES
PLANES = 3
ROWS = 56
GRP = 32
SLC = 16
ORB = 32
PAIRS = 32
HALVES = 2
CHUNKS = ((0, 40), (40, 16))
BACK_CHUNKS = ((0, 16), (16, 40))
MARGIN = 9
WIDE = 384
VMEM_LIMIT = 60 * 1024 * 1024

NEAR, OWNER, FAR, SEAT, WANT = 0, 1, 2, 3, 5
GAP, BLOCK, REST = 8, 11, 13


def split_np(values):
    high = values.astype(jnp.bfloat16)
    low = (values - high.astype(np.float64)).astype(jnp.bfloat16)
    return high, low


@functools.cache
def tables():
    k = np.arange(B, dtype=np.float64)
    q = np.sqrt(2.0 / (B + 1)) * np.sin(np.pi * np.outer(k + 1, k + 1) / (B + 1))
    lam = 2.0 - 2.0 * np.cos(np.pi * (k + 1) / (B + 1))
    plane_of = 3 * (np.arange(B) % SLC) + np.arange(B) // SLC
    q_c = np.kron(np.eye(WIDE // B), q)
    q_a = np.zeros((B, LANES))
    q_a[:, :B] = q[plane_of]
    q_high, q_low = split_np(q)
    q_b = np.concatenate([q_high, q_low, q_high], axis=1)
    lam_b = np.broadcast_to(lam[:, None], (B, 2 * LANES)).astype(np.float32)
    lane = np.arange(LANES)
    lam_a = np.where(lane < B, lam[lane % B], 1.0)
    lam_ac = np.zeros((B // 2, 1, 2 * LANES), np.float32)
    for kc in range(B):
        lam_ac[kc // 2, 0, (kc % 2) * LANES : (kc % 2 + 1) * LANES] = lam_a + lam[kc]
    return (*split_np(q_c), *split_np(q_a), q_b, lam_b, lam_ac)


def iota(shape, dim):
    return lax.broadcasted_iota(jnp.int32, shape, dim)


def total_of(mask, values, axis):
    return jnp.sum(jnp.where(mask, values, 0), axis=axis, keepdims=True)


def index_tables(owner, remote, resident, count):
    square = (PAIRS, PAIRS)
    down, across = iota(square, 0), iota(square, 1)

    def as_column(row):
        return total_of(down == across, row, 1)

    owner_col = as_column(owner)
    same = owner_col == owner
    ones = jnp.ones(square, jnp.int32)

    def places(before, axis, other_axis):
        return total_of(same & before, ones, axis), total_of(same, ones, axis)

    rank_row, times_row = places(down < across, 0, 1)
    rank_col, times_col = places(across < down, 1, 0)

    def seats(rank, times, rank_other, times_other, before, axis):
        single, first, second = times == 1, (times == 2) & (rank == 0), rank == 1
        single_o, first_o, second_o = times_other == 1, (times_other == 2) & (rank_other == 0), rank_other == 1
        twice = jnp.sum(jnp.where(second_o, 1, 0), axis=axis, keepdims=True)
        at_first = total_of(before & first_o, ones, axis)
        at_second = total_of(before & second_o, ones, axis)
        filled = twice + total_of(before & single_o, ones, axis)
        late = single & (filled >= SLC)
        half = jnp.where(second | late, 1, 0)
        seat = jnp.where(
            first, at_first, jnp.where(second, at_second, jnp.where(late, filled - SLC + twice, filled))
        )
        return half, seat

    half_row, seat_row = seats(rank_row, times_row, rank_col, times_col, down < across, 0)
    half_col, seat_col = seats(rank_col, times_col, rank_row, times_row, across < down, 1)

    upto = iota((SLC, SLC), 1) <= iota((SLC, SLC), 0)
    running = total_of(upto, count, 1)
    home = jnp.sum(jnp.where(running <= iota((SLC, PAIRS), 1), 1, 0), axis=0, keepdims=True)
    near_col = as_column(home * 2 + resident)
    remote_col = as_column(remote)

    wide = (PAIRS, LANES)
    lane = iota(wide, 1)
    seated = (half_col * SLC + seat_col) == lane
    rows = [jnp.zeros((1, LANES), jnp.int32)] * 8
    rows[NEAR] = total_of(seated, near_col + jnp.zeros(wide, jnp.int32), 0)
    rows[OWNER] = total_of(seated, owner_col + jnp.zeros(wide, jnp.int32), 0)
    rows[FAR] = total_of(seated, owner_col * ORB + remote_col + jnp.zeros(wide, jnp.int32), 0)
    requests = jnp.zeros((GRP, LANES), jnp.int32)
    for h in range(HALVES):
        named = (owner_col == lane) & (half_col == h)
        rows[SEAT + h] = total_of(named, seat_col + jnp.zeros(wide, jnp.int32), 0)
        rows[WANT + h] = ORB + total_of(named, remote_col - ORB + jnp.zeros(wide, jnp.int32), 0)
        asked = (down == owner) & (half_row == h)
        want_col = ORB + total_of(asked, remote - ORB + jnp.zeros(square, jnp.int32), 1)
        requests = jnp.where(iota((GRP, LANES), 1) == h, want_col, requests)
    for n, most in ((NEAR, ORB - 1), (OWNER, GRP - 1), (SEAT, SLC - 1), (SEAT + 1, SLC - 1), (WANT, ORB), (WANT + 1, ORB)):
        rows[n] = jnp.clip(rows[n], 0, most)
    return rows, jnp.clip(requests, 0, ORB)


def shift_rows(rows, offsets, me_g, me_s):
    lane = iota((1, LANES), 1)
    orbital = iota(offsets.shape, 1)
    rows += [jnp.zeros((1, LANES), jnp.int32) for _ in range(8)]
    for h in range(HALVES):
        mine = lane == SLC * h + me_s
        near = me_g * ORB + total_of(mine, rows[NEAR], 1)
        far = total_of(mine, rows[FAR], 1)
        gap = total_of(orbital == near, offsets, 1) - total_of(orbital == far, offsets, 1)
        for k in range(3):
            rows[GAP + k] = jnp.where(lane == h, gap[k : k + 1], rows[GAP + k])
        turn = gap[1:2] * B + gap[2:3]
        for n, sign in enumerate((1, -1)):
            reach = sign * turn + MARGIN * LANES
            reach = jnp.clip(reach, 0, (2 * MARGIN) * LANES - 1)
            block = lax.div(reach, jnp.full_like(reach, LANES))
            rows[BLOCK + n] = jnp.where(lane == h, block, rows[BLOCK + n])
            rows[REST + n] = jnp.where(lane == h, reach - block * LANES, rows[REST + n])


def stack_rows(rows):
    at = iota((len(rows), LANES), 0)
    table = jnp.zeros((len(rows), LANES), jnp.int32)
    for n, row in enumerate(rows):
        table = jnp.where(at == n, row, table)
    return table


def split(values):
    high = values.astype(jnp.bfloat16)
    return high, (values - high.astype(jnp.float32)).astype(jnp.bfloat16)


def dot(left, right, dims=((1,), (0,))):
    return lax.dot_general(left, right, (dims, ((), ())), preferred_element_type=jnp.float32)


def plane_at(shape, dim):
    row = iota(shape, dim)
    return 3 * lax.rem(row, SLC) + lax.div(row, SLC)


GROUPS = [slice(g * WIDE, (g + 1) * WIDE) for g in range(CELLS // WIDE)]


def wire_places():
    for q in range(BLOCKS):
        for p in range(PLANES):
            yield (
                pl.ds(3 * q + p, SLC, stride=ROWS),
                slice(p * SLC, (p + 1) * SLC),
                slice(q * LANES, (q + 1) * LANES),
            )


def lane_shift(blocks, block, rest):
    loaded = [blocks[block + q] for q in range(BLOCKS + 1)]
    near, over = jnp.concatenate(loaded[:-1], axis=0), jnp.concatenate(loaded[1:], axis=0)
    high, low = split(jnp.concatenate([near, over], axis=1))
    square = (2 * LANES, LANES)
    onehot = jnp.where(iota(square, 0) == iota(square, 1) + rest, 1.0, 0.0).astype(jnp.bfloat16)
    out = dot(high, onehot) + dot(low, onehot)
    return jnp.concatenate([out[q * B : (q + 1) * B] for q in range(BLOCKS)], axis=1)


def pair_fields(gap, there, back, near_box, far_box, near_field, far_field, consts, scratch):
    qc_high, qc_low, qa_high, qa_low, q_b, lam_b, lam_ac = consts
    psi, moved, blocks, modes = scratch
    e0, e1, e2 = gap
    lane = iota((8, CELLS), 1)[:1]
    at_b, at_c = lax.div(lane, B) + e1, lax.rem(lane, B) + e2
    inside = (at_b >= 0) & (at_b < B) & (at_c >= 0) & (at_c < B)
    inside = jnp.where(inside, 1.0, 0.0).astype(jnp.float32)
    onehot = jnp.where(plane_at((B, B), 0) + e0 == plane_at((B, B), 1), 1.0, 0.0).astype(jnp.bfloat16)
    for where, rows, cols in wire_places():
        psi[rows, cols] = near_box[where, :]
        blocks[MARGIN + cols.start // LANES, rows, :] = far_box[where, :]
    high, low = split(lane_shift(blocks, *there) * inside)
    moved[...] = dot(onehot, high) + dot(onehot, low)

    density = jnp.concatenate([psi[:, cols] * moved[:, cols] for cols in GROUPS], axis=0)
    high, low = split(density)
    part = dot(high, qc_high[...]) + dot(low, qc_high[...]) + dot(high, qc_low[...])
    for g, cols in enumerate(GROUPS):
        high, low = split(part[g * B : (g + 1) * B])
        over = ((0,), (0,))
        modes[cols, :] = (
            dot(high, qa_high[...], over) + dot(low, qa_high[...], over) + dot(high, qa_low[...], over)
        )

    def along_b(values):
        high, low = split(values)
        return dot(q_b[...], jnp.concatenate([high, high, low], axis=0))

    def weigh(i, _):
        even, odd = pl.ds(2 * i, B, stride=B), pl.ds(2 * i + 1, B, stride=B)
        values = along_b(jnp.concatenate([modes[even, :], modes[odd, :]], axis=1))
        values = along_b(values / (lam_b[...] + lam_ac[i]))
        modes[even, :] = values[:, :LANES]
        modes[odd, :] = values[:, LANES:]
        return 0

    lax.fori_loop(0, B // 2, weigh, 0, unroll=2)

    parts = []
    for cols in GROUPS:
        high, low = split(modes[cols, :])
        over = ((1,), (1,))
        parts.append(
            dot(qa_high[...], high, over) + dot(qa_high[...], low, over) + dot(qa_low[...], high, over)
        )
    high, low = split(jnp.concatenate(parts, axis=0))
    potential = dot(high, qc_high[...]) + dot(low, qc_high[...]) + dot(high, qc_low[...])
    for g, cols in enumerate(GROUPS):
        here = potential[g * B : (g + 1) * B]
        moved[:, cols] = here * moved[:, cols]
        high, low = split(here * psi[:, cols] * inside[:, cols])
        over = ((0,), (0,))
        apart = dot(onehot, high, over) + dot(onehot, low, over)
        for n in range(WIDE // LANES):
            blocks[MARGIN + cols.start // LANES + n] = apart[:, n * LANES : (n + 1) * LANES]
    far = lane_shift(blocks, *back)
    for where, rows, cols in wire_places():
        near_field[where, :] = moved[rows, cols]
        far_field[where, :] = far[rows, cols]


def peer(me, i, count):
    return lax.rem(me + (i // 2 + 1) * (1 - 2 * (i % 2)) + count, count)


def part_of(slot, count):
    return pl.ds(pl.multiple_of(slot * count, 8), count)


def rows_of(slot, row, count):
    return pl.ds(pl.multiple_of(slot * ROWS + row, 8), count)


N = len(CHUNKS)


def exchange_kernel(*refs):
    names = iter(refs)

    def take(count=1):
        out = [next(names) for _ in range(count)]
        return out[0] if count == 1 else out

    def halves():
        return take(HALVES)

    def chunked():
        return [take(N) for _ in range(HALVES)]

    owner, remote, resident, count_row, offsets, orb_hbm = take(6)
    consts_hbm = take(7)
    near_back, answers = halves(), halves()
    table_out, req_recv = take(2)
    orb, slabs, want, table_smem, req_smem = take(5)
    consts = take(7)
    near_send, near_box, far_box, near_field, far_field = (halves() for _ in range(5))
    g_send, g_recv, f_send, f_back, a_send = (chunked() for _ in range(5))
    scratch = take(4)
    local_sem, const_sem, rq_s, rq_r, near_s, near_r, nback_s, nback_r = take(8)
    grp_s, grp_r, far_s, far_r, fback_s, fback_r, ans_s, ans_r = take(8)

    me_g, me_s = lax.axis_index("grp"), lax.axis_index("slc")

    def each(axis, action):
        me, count = (me_g, GRP) if axis == "grp" else (me_s, SLC)

        def step(i, _):
            action(peer(me, i, count))
            return 0

        lax.fori_loop(0, count - 1, step, 0)

    orb_copy = pltpu.make_async_copy(orb_hbm, orb, local_sem.at[2])
    orb_copy.start()
    const_copies = [pltpu.make_async_copy(a, b, const_sem.at[n]) for n, (a, b) in enumerate(zip(consts_hbm, consts))]
    for copy in const_copies:
        copy.start()
    barrier = pltpu.get_barrier_semaphore()
    each("grp", lambda there: pl.semaphore_signal(barrier, inc=1, device_id={"grp": there}))
    each("slc", lambda there: pl.semaphore_signal(barrier, inc=1, device_id={"slc": there}))

    rows, requests = index_tables(owner[...], remote[...], resident[...], count_row[...])
    shift_rows(rows, offsets[...], me_g, me_s)
    table_out[...] = stack_rows(rows)
    want[...] = requests.reshape(GRP, 1, LANES)
    local = pltpu.make_async_copy(table_out, table_smem, local_sem.at[0])
    local.start()
    orb_copy.wait()
    for q in range(BLOCKS):
        for p in range(PLANES):
            slabs[:ORB, 3 * q + p, :] = orb[p, :, q * LANES : (q + 1) * LANES]
    slabs[:ORB, 54:56, :] = jnp.zeros((ORB, 2, LANES), jnp.float32)
    slabs[ORB] = jnp.zeros((ROWS, LANES), jnp.float32)
    blocks = scratch[2]
    blocks[...] = jnp.zeros_like(blocks)
    local.wait()
    pl.semaphore_wait(barrier, GRP + SLC - 2)

    def remote_copy(src, dst, send, recv, axis, there):
        return pltpu.make_async_remote_copy(
            src_ref=src, dst_ref=dst, send_sem=send, recv_sem=recv, device_id={axis: there}
        )

    def req_copy(there, slot):
        return remote_copy(want.at[there], req_recv.at[slot], rq_s.at[0], rq_r.at[0], "grp", there)

    def near_copy(h, there, slot):
        return remote_copy(
            near_send[h].at[part_of(there, ROWS)], near_box[h].at[part_of(slot, ROWS)],
            near_s.at[h], near_r.at[h], "slc", there,
        )

    def grp_copy(h, c, there, slot):
        return remote_copy(
            g_send[h][c].at[there], g_recv[h][c].at[slot], grp_s.at[N * h + c], grp_r.at[N * h + c], "grp", there
        )

    def far_copy(h, c, there, slot):
        row, count = CHUNKS[c]
        return remote_copy(
            f_send[h][c].at[there], far_box[h].at[rows_of(slot, row, count)],
            far_s.at[N * h + c], far_r.at[N * h + c], "slc", there,
        )

    def fback_copy(h, c, there, slot):
        row, count = BACK_CHUNKS[c]
        return remote_copy(
            far_field[h].at[rows_of(there, row, count)], f_back[h][c].at[slot],
            fback_s.at[N * h + c], fback_r.at[N * h + c], "slc", there,
        )

    def nback_copy(h, there, slot):
        return remote_copy(
            near_field[h].at[part_of(there, ROWS)], near_back[h].at[part_of(slot, ROWS)],
            nback_s.at[h], nback_r.at[h], "slc", there,
        )

    def ans_copy(h, c, there, slot):
        row, count = BACK_CHUNKS[c]
        return remote_copy(
            a_send[h][c].at[there], answers[h].at[rows_of(slot, row, count)],
            ans_s.at[N * h + c], ans_r.at[N * h + c], "grp", there,
        )

    def all_of(ref, size, send, recv, axis):
        me, count = (me_g, GRP) if axis == "grp" else (me_s, SLC)
        whole = ref.at[pl.ds(0, size)]
        return remote_copy(whole, whole, send, recv, axis, peer(me, 0, count))

    def all_req():
        return all_of(req_recv, GRP - 1, rq_s.at[0], rq_r.at[0], "grp")

    def all_near(h):
        return all_of(near_box[h], (SLC - 1) * ROWS, near_s.at[h], near_r.at[h], "slc")

    def all_grp(h, c):
        return all_of(g_recv[h][c], GRP - 1, grp_s.at[N * h + c], grp_r.at[N * h + c], "grp")

    def all_far(h, c):
        return all_of(f_send[h][c], SLC - 1, far_s.at[N * h + c], far_r.at[N * h + c], "slc")

    def all_fback(h, c):
        return all_of(f_back[h][c], SLC - 1, fback_s.at[N * h + c], fback_r.at[N * h + c], "slc")

    def all_nback(h):
        return all_of(near_back[h], (SLC - 1) * ROWS, nback_s.at[h], nback_r.at[h], "slc")

    def all_ans(h, c):
        return all_of(a_send[h][c], GRP - 1, ans_s.at[N * h + c], ans_r.at[N * h + c], "grp")

    def send_near(h):
        def one(there):
            near_send[h][part_of(there, ROWS), :] = slabs[table_smem[NEAR, SLC * h + there]]
            near_copy(h, there, me_s).start()

        each("slc", one)
        near_box[h][part_of(me_s, ROWS), :] = slabs[table_smem[NEAR, SLC * h + me_s]]

    def send_grp(h, c):
        row, count = CHUNKS[c]

        def one(there):
            g_send[h][c][there] = slabs[req_smem[there, 0, h], row : row + count, :]
            grp_copy(h, c, there, me_g).start()

        each("grp", one)
        g_recv[h][c][me_g] = slabs[table_smem[WANT + h, me_g], row : row + count, :]

    def forward_far(h, c):
        row, count = CHUNKS[c]
        all_grp(h, c).wait_recv()

        def one(there):
            f_send[h][c][there] = g_recv[h][c][table_smem[OWNER, SLC * h + there]]
            far_copy(h, c, there, me_s).start()

        each("slc", one)
        far_box[h][rows_of(me_s, row, count), :] = g_recv[h][c][table_smem[OWNER, SLC * h + me_s]]

    def await_boxes(h):
        all_near(h).wait_recv()
        for c in range(N):
            all_far(h, c).wait_recv()

    def compute(h):
        gap = [table_smem[GAP + k, h] for k in range(3)]
        there, back = [(table_smem[BLOCK + n, h], table_smem[REST + n, h]) for n in range(2)]
        pair_fields(gap, there, back, near_box[h], far_box[h], near_field[h], far_field[h], consts, scratch)

    def send_fields(h):
        for c, (row, count) in enumerate(BACK_CHUNKS):
            if c:
                all_fback(h, c - 1).wait_send()
            each("slc", lambda there: fback_copy(h, c, there, me_s).start())
            f_back[h][c][me_s] = far_field[h][rows_of(me_s, row, count), :]

    def send_near_fields(h):
        each("slc", lambda there: nback_copy(h, there, me_s).start())
        near_back[h][part_of(me_s, ROWS), :] = near_field[h][part_of(me_s, ROWS), :]

    def send_answers(h, c):
        row, count = BACK_CHUNKS[c]
        all_fback(h, c).wait_recv()

        def one(there):
            a_send[h][c][there] = f_back[h][c][table_smem[SEAT + h, there]]
            ans_copy(h, c, there, me_g).start()

        each("grp", one)
        answers[h][rows_of(me_g, row, count), :] = f_back[h][c][table_smem[SEAT + h, me_g]]

    each("grp", lambda there: req_copy(there, me_g).start())
    req_recv[me_g] = want[me_g]
    send_near(0)
    all_req().wait_recv()
    asked = pltpu.make_async_copy(req_recv, req_smem, local_sem.at[1])
    asked.start()
    asked.wait()
    send_grp(0, 0)
    send_near(1)
    all_grp(0, 0).wait_send()
    send_grp(0, 1)
    forward_far(0, 0)
    send_grp(1, 0)
    forward_far(0, 1)
    for copy in const_copies:
        copy.wait()
    await_boxes(0)
    send_grp(1, 1)
    compute(0)
    send_fields(0)
    for c in range(N):
        forward_far(1, c)
        send_answers(0, c)
    await_boxes(1)
    send_near_fields(0)
    compute(1)
    send_fields(1)
    for c in range(N):
        send_answers(1, c)
    send_near_fields(1)

    all_req().wait_send()
    for h in range(HALVES):
        all_near(h).wait_send()
        all_nback(h).wait()
        all_fback(h, N - 1).wait_send()
        for c in range(N):
            if (h, c) != (0, 0):
                all_grp(h, c).wait_send()
            all_far(h, c).wait_send()
            all_ans(h, c).wait()


def exchange(owner, remote, resident, count, offsets, orb):
    vmem = pl.BlockSpec(memory_space=pltpu.VMEM)

    def slots(number):
        return pltpu.VMEM((number * ROWS, LANES), jnp.float32)

    def out(number):
        return jax.ShapeDtypeStruct((number * ROWS, LANES), jnp.float32)

    def chunked(number, chunks):
        return [pltpu.VMEM((number, rows, LANES), jnp.float32) for _ in range(HALVES) for _, rows in chunks]

    hbm = pl.BlockSpec(memory_space=pltpu.HBM)
    consts = [jnp.asarray(t) for t in tables()]

    def sems(number):
        return [pltpu.SemaphoreType.DMA((number,))] * 2

    return pl.pallas_call(
        exchange_kernel,
        out_shape=[
            *[out(SLC)] * HALVES,
            *[out(GRP)] * HALVES,
            jax.ShapeDtypeStruct((16, LANES), jnp.int32),
            jax.ShapeDtypeStruct((GRP, 1, LANES), jnp.int32),
        ],
        in_specs=[vmem, vmem, vmem, vmem, vmem, hbm, *[hbm] * len(consts)],
        out_specs=[vmem] * 6,
        scratch_shapes=[
            pltpu.VMEM(orb.shape, jnp.float32),
            pltpu.VMEM((ORB + 1, ROWS, LANES), jnp.float32),
            pltpu.VMEM((GRP, 1, LANES), jnp.int32),
            pltpu.SMEM((16, LANES), jnp.int32),
            pltpu.SMEM((GRP, 1, LANES), jnp.int32),
            *[pltpu.VMEM(t.shape, t.dtype) for t in consts],
            *[slots(SLC)] * (5 * HALVES),
            *chunked(GRP, CHUNKS),
            *chunked(GRP, CHUNKS),
            *chunked(SLC, CHUNKS),
            *chunked(SLC, BACK_CHUNKS),
            *chunked(GRP, BACK_CHUNKS),
            *[pltpu.VMEM((B, CELLS), jnp.float32)] * 2,
            pltpu.VMEM((2 * MARGIN + BLOCKS, B, LANES), jnp.float32),
            pltpu.VMEM((CELLS, LANES), jnp.float32),
            pltpu.SemaphoreType.DMA((3,)),
            pltpu.SemaphoreType.DMA((len(consts),)),
            *sems(1),
            *sems(HALVES),
            *sems(HALVES),
            *sems(HALVES * N),
            *sems(HALVES * N),
            *sems(HALVES * N),
            *sems(HALVES * N),
        ],
        compiler_params=pltpu.CompilerParams(
            collective_id=0, has_side_effects=True, vmem_limit_bytes=VMEM_LIMIT
        ),
        name="exchange",
    )(owner, remote, resident, count, offsets, orb, *consts)


def sum_kernel(table, requested, orb_hbm, pot_hbm, near_0, near_1, answers_0, answers_1, out, total, orb, pot, sem):
    copies = [
        pltpu.make_async_copy(orb_hbm, orb, sem.at[0]),
        pltpu.make_async_copy(pot_hbm, pot, sem.at[1]),
    ]
    for copy in copies:
        copy.start()
    total[...] = jnp.zeros_like(total)

    def add(source, t, place):
        total[part_of(place, ROWS), :] += source[part_of(t, ROWS), :]

    def add_near(t, _):
        add(near_0, t, table[NEAR, t])
        add(near_1, t, table[NEAR, SLC + t])
        return 0

    def add_far(t, _):
        add(answers_0, t, requested[t, 0, 0])
        add(answers_1, t, requested[t, 0, 1])
        return 0

    lax.fori_loop(0, SLC, add_near, 0)
    lax.fori_loop(0, GRP, add_far, 0)
    for copy in copies:
        copy.wait()
    for q in range(BLOCKS):
        for p in range(PLANES):
            cols = slice(q * LANES, (q + 1) * LANES)
            field = total[pl.ds(3 * q + p, ORB, stride=ROWS), :]
            out[p, :, cols] = pot[p, :, cols] * orb[p, :, cols] - field


def sums(table, requested, orb, pot, fields):
    smem, vmem = pl.BlockSpec(memory_space=pltpu.SMEM), pl.BlockSpec(memory_space=pltpu.VMEM)
    return pl.pallas_call(
        sum_kernel,
        out_shape=jax.ShapeDtypeStruct(orb.shape, jnp.float32),
        in_specs=[smem, smem, *[pl.BlockSpec(memory_space=pltpu.HBM)] * 2, *[vmem] * 4],
        out_specs=vmem,
        scratch_shapes=[
            pltpu.VMEM(((ORB + 1) * ROWS, LANES), jnp.float32),
            *[pltpu.VMEM(orb.shape, jnp.float32)] * 2,
            pltpu.SemaphoreType.DMA((2,)),
        ],
        compiler_params=pltpu.CompilerParams(vmem_limit_bytes=VMEM_LIMIT),
        name="sums",
    )(table, requested, orb, pot, *fields)


def per_device(orbitals, local_pot, pair_owner, pair_remote, pair_resident, pair_count, offsets):
    orb, pot = jnp.transpose(orbitals, (1, 0, 2)), jnp.transpose(local_pot, (1, 0, 2))
    *fields, table, requested = exchange(
        pair_owner.reshape(1, PAIRS), pair_remote, pair_resident, pair_count, offsets.T, orb
    )
    return jnp.transpose(sums(table, requested, orb, pot, fields), (1, 0, 2))


def solution(mesh):
    in_specs = (
        P("grp", "slc", None),
        P("grp", "slc", None),
        P("grp", None, None),
        P("grp", None),
        P("grp", None),
        P("grp", None),
        P(),
    )
    return jax.shard_map(
        per_device, mesh=mesh, in_specs=in_specs, out_specs=P("grp", "slc", None), check_vma=False
    )
```

```python
import functools

import jax
import jax.numpy as jnp
import numpy as np
from jax import lax
from jax.experimental import pallas as pl
from jax.experimental.pallas import tpu as pltpu
from jax.sharding import PartitionSpec as P

B = 48
CELLS = B * B
LANES = 128
BLOCKS = CELLS // LANES
PLANES = 3
ROWS = 56
GRP = 32
SLC = 16
ORB = 32
PAIRS = 32
HALVES = 2
CHUNKS = ((0, 40), (40, 16))
BACK_CHUNKS = ((0, 16), (16, 40))
MARGIN = 9
WIDE = 384
PART = 256
HELD = WIDE // 2
VMEM_LIMIT = 60 * 1024 * 1024

NEAR, OWNER, FAR, SEAT, WANT = 0, 1, 2, 3, 5
GAP, BLOCK, REST = 8, 11, 13


def split_np(values):
    high = values.astype(jnp.bfloat16)
    low = (values - high.astype(np.float64)).astype(jnp.bfloat16)
    return high, low


@functools.cache
def tables():
    k = np.arange(B, dtype=np.float64)
    q = np.sqrt(2.0 / (B + 1)) * np.sin(np.pi * np.outer(k + 1, k + 1) / (B + 1))
    lam = 2.0 - 2.0 * np.cos(np.pi * (k + 1) / (B + 1))
    plane_of = 3 * (np.arange(B) % SLC) + np.arange(B) // SLC
    q_c = np.zeros((WIDE, 2 * PART))
    for b in range(WIDE // B):
        for c in range(B):
            q_c[b * B : (b + 1) * B, PART * (c % 2) + b * (B // 2) + c // 2] = q[:, c]
    q_a = np.zeros((2 * B, LANES))
    q_a[:B, :B] = q[plane_of]
    q_a[B:, LANES // 2 : LANES // 2 + B] = q[plane_of]
    q_high, q_low = split_np(q)
    q_b = np.concatenate([q_high, q_low, q_high], axis=1)
    lam_b = np.broadcast_to(lam[:, None], (B, 2 * LANES)).astype(np.float32)
    lam_ac = np.ones((B // 4, 1, 2 * LANES), np.float32)
    for kc in range(B):
        start = (kc // 2 % 2) * LANES + (kc % 2) * (LANES // 2)
        lam_ac[kc // 4, 0, start : start + B] = lam + lam[kc]
    return (*split_np(q_c), *split_np(q_a), q_b, lam_b, lam_ac)


def iota(shape, dim):
    return lax.broadcasted_iota(jnp.int32, shape, dim)


def total_of(mask, values, axis):
    return jnp.sum(jnp.where(mask, values, 0), axis=axis, keepdims=True)


def index_tables(owner, remote, resident, count):
    square = (PAIRS, PAIRS)
    down, across = iota(square, 0), iota(square, 1)

    def as_column(row):
        return total_of(down == across, row, 1)

    owner_col = as_column(owner)
    same = owner_col == owner
    ones = jnp.ones(square, jnp.int32)

    def places(before, axis, other_axis):
        return total_of(same & before, ones, axis), total_of(same, ones, axis)

    rank_row, times_row = places(down < across, 0, 1)
    rank_col, times_col = places(across < down, 1, 0)

    def seats(rank, times, rank_other, times_other, before, axis):
        single, first, second = times == 1, (times == 2) & (rank == 0), rank == 1
        single_o, first_o, second_o = times_other == 1, (times_other == 2) & (rank_other == 0), rank_other == 1
        twice = jnp.sum(jnp.where(second_o, 1, 0), axis=axis, keepdims=True)
        at_first = total_of(before & first_o, ones, axis)
        at_second = total_of(before & second_o, ones, axis)
        filled = twice + total_of(before & single_o, ones, axis)
        late = single & (filled >= SLC)
        half = jnp.where(second | late, 1, 0)
        seat = jnp.where(
            first, at_first, jnp.where(second, at_second, jnp.where(late, filled - SLC + twice, filled))
        )
        return half, seat

    half_row, seat_row = seats(rank_row, times_row, rank_col, times_col, down < across, 0)
    half_col, seat_col = seats(rank_col, times_col, rank_row, times_row, across < down, 1)

    upto = iota((SLC, SLC), 1) <= iota((SLC, SLC), 0)
    running = total_of(upto, count, 1)
    home = jnp.sum(jnp.where(running <= iota((SLC, PAIRS), 1), 1, 0), axis=0, keepdims=True)
    near_col = as_column(home * 2 + resident)
    remote_col = as_column(remote)

    wide = (PAIRS, LANES)
    lane = iota(wide, 1)
    seated = (half_col * SLC + seat_col) == lane
    rows = [jnp.zeros((1, LANES), jnp.int32)] * 8
    rows[NEAR] = total_of(seated, near_col + jnp.zeros(wide, jnp.int32), 0)
    rows[OWNER] = total_of(seated, owner_col + jnp.zeros(wide, jnp.int32), 0)
    rows[FAR] = total_of(seated, owner_col * ORB + remote_col + jnp.zeros(wide, jnp.int32), 0)
    requests = jnp.zeros((GRP, LANES), jnp.int32)
    for h in range(HALVES):
        named = (owner_col == lane) & (half_col == h)
        rows[SEAT + h] = total_of(named, seat_col + jnp.zeros(wide, jnp.int32), 0)
        rows[WANT + h] = ORB + total_of(named, remote_col - ORB + jnp.zeros(wide, jnp.int32), 0)
        asked = (down == owner) & (half_row == h)
        want_col = ORB + total_of(asked, remote - ORB + jnp.zeros(square, jnp.int32), 1)
        requests = jnp.where(iota((GRP, LANES), 1) == h, want_col, requests)
    for n, most in ((NEAR, ORB - 1), (OWNER, GRP - 1), (SEAT, SLC - 1), (SEAT + 1, SLC - 1), (WANT, ORB), (WANT + 1, ORB)):
        rows[n] = jnp.clip(rows[n], 0, most)
    return rows, jnp.clip(requests, 0, ORB)


def shift_rows(rows, offsets, me_g, me_s):
    lane = iota((1, LANES), 1)
    orbital = iota(offsets.shape, 1)
    rows += [jnp.zeros((1, LANES), jnp.int32) for _ in range(8)]
    for h in range(HALVES):
        mine = lane == SLC * h + me_s
        near = me_g * ORB + total_of(mine, rows[NEAR], 1)
        far = total_of(mine, rows[FAR], 1)
        gap = total_of(orbital == near, offsets, 1) - total_of(orbital == far, offsets, 1)
        for k in range(3):
            rows[GAP + k] = jnp.where(lane == h, gap[k : k + 1], rows[GAP + k])
        turn = gap[1:2] * B + gap[2:3]
        for n, sign in enumerate((1, -1)):
            reach = sign * turn + MARGIN * LANES
            reach = jnp.clip(reach, 0, (2 * MARGIN) * LANES - 1)
            block = lax.div(reach, jnp.full_like(reach, LANES))
            rows[BLOCK + n] = jnp.where(lane == h, block, rows[BLOCK + n])
            rows[REST + n] = jnp.where(lane == h, reach - block * LANES, rows[REST + n])


def stack_rows(rows):
    at = iota((len(rows), LANES), 0)
    table = jnp.zeros((len(rows), LANES), jnp.int32)
    for n, row in enumerate(rows):
        table = jnp.where(at == n, row, table)
    return table


def split(values):
    high = values.astype(jnp.bfloat16)
    return high, (values - high.astype(jnp.float32)).astype(jnp.bfloat16)


def dot(left, right, dims=((1,), (0,))):
    return lax.dot_general(left, right, (dims, ((), ())), preferred_element_type=jnp.float32)


def plane_at(shape, dim):
    row = iota(shape, dim)
    return 3 * lax.rem(row, SLC) + lax.div(row, SLC)


GROUPS = [slice(g * WIDE, (g + 1) * WIDE) for g in range(CELLS // WIDE)]


def wire_places():
    for q in range(BLOCKS):
        for p in range(PLANES):
            yield (
                pl.ds(3 * q + p, SLC, stride=ROWS),
                slice(p * SLC, (p + 1) * SLC),
                slice(q * LANES, (q + 1) * LANES),
            )


def lane_shift(blocks, block, rest):
    loaded = [blocks[block + q] for q in range(BLOCKS + 1)]
    near, over = jnp.concatenate(loaded[:-1], axis=0), jnp.concatenate(loaded[1:], axis=0)
    high, low = split(jnp.concatenate([near, over], axis=1))
    square = (2 * LANES, LANES)
    onehot = jnp.where(iota(square, 0) == iota(square, 1) + rest, 1.0, 0.0).astype(jnp.bfloat16)
    out = dot(high, onehot) + dot(low, onehot)
    return jnp.concatenate([out[q * B : (q + 1) * B] for q in range(BLOCKS)], axis=1)


def pair_fields(gap, there, back, near_box, far_box, near_field, far_field, consts, scratch):
    qc_high, qc_low, qa_high, qa_low, q_b, lam_b, lam_ac = consts
    psi, moved, blocks, modes = scratch
    e0, e1, e2 = gap
    lane = iota((8, CELLS), 1)[:1]
    at_b, at_c = lax.div(lane, B) + e1, lax.rem(lane, B) + e2
    inside = (at_b >= 0) & (at_b < B) & (at_c >= 0) & (at_c < B)
    inside = jnp.where(inside, 1.0, 0.0).astype(jnp.float32)
    onehot = jnp.where(plane_at((B, B), 0) + e0 == plane_at((B, B), 1), 1.0, 0.0).astype(jnp.bfloat16)
    for where, rows, cols in wire_places():
        psi[rows, cols] = near_box[where, :]
        blocks[MARGIN + cols.start // LANES, rows, :] = far_box[where, :]
    high, low = split(lane_shift(blocks, *there) * inside)
    moved[...] = dot(onehot, high) + dot(onehot, low)

    density = jnp.concatenate([psi[:, cols] * moved[:, cols] for cols in GROUPS], axis=0)
    high, low = split(density)
    part = dot(high, qc_high[...]) + dot(low, qc_high[...]) + dot(high, qc_low[...])
    for g in range(len(GROUPS)):
        mine = part[g * B : (g + 1) * B]
        high, low = split(jnp.concatenate([mine[:, :PART], mine[:, PART:]], axis=0))
        over = ((0,), (0,))
        out = dot(high, qa_high[...], over) + dot(low, qa_high[...], over) + dot(high, qa_low[...], over)
        modes[g * HELD : (g + 1) * HELD, :] = out[:HELD]

    def along_b(values):
        high, low = split(values)
        return dot(q_b[...], jnp.concatenate([high, high, low], axis=0))

    def weigh(i, _):
        left, right = pl.ds(2 * i, B, stride=B // 2), pl.ds(2 * i + 1, B, stride=B // 2)
        values = along_b(jnp.concatenate([modes[left, :], modes[right, :]], axis=1))
        values = along_b(values / (lam_b[...] + lam_ac[i]))
        modes[left, :] = values[:, :LANES]
        modes[right, :] = values[:, LANES:]
        return 0

    lax.fori_loop(0, B // 4, weigh, 0, unroll=4)

    parts = []
    over = ((1,), (1,))
    for g in range(len(GROUPS)):
        high, low = split(modes[g * HELD : g * HELD + PART, :])
        out = dot(qa_high[...], high, over) + dot(qa_high[...], low, over) + dot(qa_low[...], high, over)
        parts.append(jnp.concatenate([out[:B], out[B:]], axis=1))
    high, low = split(jnp.concatenate(parts, axis=0))
    potential = dot(high, qc_high[...], over) + dot(low, qc_high[...], over) + dot(high, qc_low[...], over)
    for g, cols in enumerate(GROUPS):
        here = potential[g * B : (g + 1) * B]
        moved[:, cols] = here * moved[:, cols]
        high, low = split(here * psi[:, cols] * inside[:, cols])
        over = ((0,), (0,))
        apart = dot(onehot, high, over) + dot(onehot, low, over)
        for n in range(WIDE // LANES):
            blocks[MARGIN + cols.start // LANES + n] = apart[:, n * LANES : (n + 1) * LANES]
    far = lane_shift(blocks, *back)
    for where, rows, cols in wire_places():
        near_field[where, :] = moved[rows, cols]
        far_field[where, :] = far[rows, cols]


def peer(me, i, count):
    return lax.rem(me + (i // 2 + 1) * (1 - 2 * (i % 2)) + count, count)


def part_of(slot, count):
    return pl.ds(pl.multiple_of(slot * count, 8), count)


def rows_of(slot, row, count):
    return pl.ds(pl.multiple_of(slot * ROWS + row, 8), count)


N = len(CHUNKS)


def exchange_kernel(*refs):
    names = iter(refs)

    def take(count=1):
        out = [next(names) for _ in range(count)]
        return out[0] if count == 1 else out

    def halves():
        return take(HALVES)

    def chunked():
        return [take(N) for _ in range(HALVES)]

    owner, remote, resident, count_row, offsets, orb_hbm = take(6)
    consts_hbm = take(7)
    near_back, answers = halves(), halves()
    table_out, req_recv = take(2)
    orb, slabs, want, table_smem, req_smem = take(5)
    consts = take(7)
    near_send, near_box, far_box, near_field, far_field = (halves() for _ in range(5))
    g_send, g_recv, f_send, f_back, a_send = (chunked() for _ in range(5))
    scratch = take(4)
    local_sem, const_sem, rq_s, rq_r, near_s, near_r, nback_s, nback_r = take(8)
    grp_s, grp_r, far_s, far_r, fback_s, fback_r, ans_s, ans_r = take(8)

    me_g, me_s = lax.axis_index("grp"), lax.axis_index("slc")

    def each(axis, action):
        me, count = (me_g, GRP) if axis == "grp" else (me_s, SLC)

        def step(i, _):
            action(peer(me, i, count))
            return 0

        lax.fori_loop(0, count - 1, step, 0)

    orb_copy = pltpu.make_async_copy(orb_hbm, orb, local_sem.at[2])
    orb_copy.start()
    const_copies = [pltpu.make_async_copy(a, b, const_sem.at[n]) for n, (a, b) in enumerate(zip(consts_hbm, consts))]
    for copy in const_copies:
        copy.start()
    barrier = pltpu.get_barrier_semaphore()
    each("grp", lambda there: pl.semaphore_signal(barrier, inc=1, device_id={"grp": there}))
    each("slc", lambda there: pl.semaphore_signal(barrier, inc=1, device_id={"slc": there}))

    rows, requests = index_tables(owner[...], remote[...], resident[...], count_row[...])
    shift_rows(rows, offsets[...], me_g, me_s)
    table_out[...] = stack_rows(rows)
    want[...] = requests.reshape(GRP, 1, LANES)
    local = pltpu.make_async_copy(table_out, table_smem, local_sem.at[0])
    local.start()
    orb_copy.wait()
    for q in range(BLOCKS):
        for p in range(PLANES):
            slabs[:ORB, 3 * q + p, :] = orb[p, :, q * LANES : (q + 1) * LANES]
    slabs[:ORB, 54:56, :] = jnp.zeros((ORB, 2, LANES), jnp.float32)
    slabs[ORB] = jnp.zeros((ROWS, LANES), jnp.float32)
    blocks = scratch[2]
    blocks[...] = jnp.zeros_like(blocks)
    scratch[3][CELLS // 2 :, :] = jnp.zeros((PART - HELD, LANES), jnp.float32)
    local.wait()
    pl.semaphore_wait(barrier, GRP + SLC - 2)

    def remote_copy(src, dst, send, recv, axis, there):
        return pltpu.make_async_remote_copy(
            src_ref=src, dst_ref=dst, send_sem=send, recv_sem=recv, device_id={axis: there}
        )

    def req_copy(there, slot):
        return remote_copy(want.at[there], req_recv.at[slot], rq_s.at[0], rq_r.at[0], "grp", there)

    def near_copy(h, there, slot):
        return remote_copy(
            near_send[h].at[part_of(there, ROWS)], near_box[h].at[part_of(slot, ROWS)],
            near_s.at[h], near_r.at[h], "slc", there,
        )

    def grp_copy(h, c, there, slot):
        return remote_copy(
            g_send[h][c].at[there], g_recv[h][c].at[slot], grp_s.at[N * h + c], grp_r.at[N * h + c], "grp", there
        )

    def far_copy(h, c, there, slot):
        row, count = CHUNKS[c]
        return remote_copy(
            f_send[h][c].at[there], far_box[h].at[rows_of(slot, row, count)],
            far_s.at[N * h + c], far_r.at[N * h + c], "slc", there,
        )

    def fback_copy(h, c, there, slot):
        row, count = BACK_CHUNKS[c]
        return remote_copy(
            far_field[h].at[rows_of(there, row, count)], f_back[h][c].at[slot],
            fback_s.at[N * h + c], fback_r.at[N * h + c], "slc", there,
        )

    def nback_copy(h, there, slot):
        return remote_copy(
            near_field[h].at[part_of(there, ROWS)], near_back[h].at[part_of(slot, ROWS)],
            nback_s.at[h], nback_r.at[h], "slc", there,
        )

    def ans_copy(h, c, there, slot):
        row, count = BACK_CHUNKS[c]
        return remote_copy(
            a_send[h][c].at[there], answers[h].at[rows_of(slot, row, count)],
            ans_s.at[N * h + c], ans_r.at[N * h + c], "grp", there,
        )

    def all_of(ref, size, send, recv, axis):
        me, count = (me_g, GRP) if axis == "grp" else (me_s, SLC)
        whole = ref.at[pl.ds(0, size)]
        return remote_copy(whole, whole, send, recv, axis, peer(me, 0, count))

    def all_req():
        return all_of(req_recv, GRP - 1, rq_s.at[0], rq_r.at[0], "grp")

    def all_near(h):
        return all_of(near_box[h], (SLC - 1) * ROWS, near_s.at[h], near_r.at[h], "slc")

    def all_grp(h, c):
        return all_of(g_recv[h][c], GRP - 1, grp_s.at[N * h + c], grp_r.at[N * h + c], "grp")

    def all_far(h, c):
        return all_of(f_send[h][c], SLC - 1, far_s.at[N * h + c], far_r.at[N * h + c], "slc")

    def all_fback(h, c):
        return all_of(f_back[h][c], SLC - 1, fback_s.at[N * h + c], fback_r.at[N * h + c], "slc")

    def all_nback(h):
        return all_of(near_back[h], (SLC - 1) * ROWS, nback_s.at[h], nback_r.at[h], "slc")

    def all_ans(h, c):
        return all_of(a_send[h][c], GRP - 1, ans_s.at[N * h + c], ans_r.at[N * h + c], "grp")

    def send_near(h):
        def one(there):
            near_send[h][part_of(there, ROWS), :] = slabs[table_smem[NEAR, SLC * h + there]]
            near_copy(h, there, me_s).start()

        each("slc", one)
        near_box[h][part_of(me_s, ROWS), :] = slabs[table_smem[NEAR, SLC * h + me_s]]

    def send_grp(h, c):
        row, count = CHUNKS[c]

        def one(there):
            g_send[h][c][there] = slabs[req_smem[there, 0, h], row : row + count, :]
            grp_copy(h, c, there, me_g).start()

        each("grp", one)
        g_recv[h][c][me_g] = slabs[table_smem[WANT + h, me_g], row : row + count, :]

    def forward_far(h, c):
        row, count = CHUNKS[c]
        all_grp(h, c).wait_recv()

        def one(there):
            f_send[h][c][there] = g_recv[h][c][table_smem[OWNER, SLC * h + there]]
            far_copy(h, c, there, me_s).start()

        each("slc", one)
        far_box[h][rows_of(me_s, row, count), :] = g_recv[h][c][table_smem[OWNER, SLC * h + me_s]]

    def compute(h):
        all_near(h).wait_recv()
        for c in range(N):
            all_far(h, c).wait_recv()
        gap = [table_smem[GAP + k, h] for k in range(3)]
        there, back = [(table_smem[BLOCK + n, h], table_smem[REST + n, h]) for n in range(2)]
        pair_fields(gap, there, back, near_box[h], far_box[h], near_field[h], far_field[h], consts, scratch)

    def send_fields(h):
        for c, (row, count) in enumerate(BACK_CHUNKS):
            each("slc", lambda there: fback_copy(h, c, there, me_s).start())
            f_back[h][c][me_s] = far_field[h][rows_of(me_s, row, count), :]

    def send_near_fields(h):
        each("slc", lambda there: nback_copy(h, there, me_s).start())
        near_back[h][part_of(me_s, ROWS), :] = near_field[h][part_of(me_s, ROWS), :]

    def send_answers(h, c):
        row, count = BACK_CHUNKS[c]
        all_fback(h, c).wait_recv()

        def one(there):
            a_send[h][c][there] = f_back[h][c][table_smem[SEAT + h, there]]
            ans_copy(h, c, there, me_g).start()

        each("grp", one)
        answers[h][rows_of(me_g, row, count), :] = f_back[h][c][table_smem[SEAT + h, me_g]]

    each("grp", lambda there: req_copy(there, me_g).start())
    req_recv[me_g] = want[me_g]
    send_near(0)
    all_req().wait_recv()
    asked = pltpu.make_async_copy(req_recv, req_smem, local_sem.at[1])
    asked.start()
    asked.wait()
    for c in range(N):
        send_grp(0, c)
    send_near(1)
    for c in range(N):
        forward_far(0, c)
        send_grp(1, c)
    for copy in const_copies:
        copy.wait()
    compute(0)
    send_fields(0)
    for c in range(N):
        forward_far(1, c)
        send_answers(0, c)
    send_near_fields(0)
    compute(1)
    send_fields(1)
    for c in range(N):
        send_answers(1, c)
    send_near_fields(1)

    all_req().wait_send()
    for h in range(HALVES):
        all_near(h).wait_send()
        all_nback(h).wait()
        for c in range(N):
            all_grp(h, c).wait_send()
            all_far(h, c).wait_send()
            all_fback(h, c).wait_send()
            all_ans(h, c).wait()


def exchange(owner, remote, resident, count, offsets, orb):
    vmem = pl.BlockSpec(memory_space=pltpu.VMEM)

    def slots(number):
        return pltpu.VMEM((number * ROWS, LANES), jnp.float32)

    def out(number):
        return jax.ShapeDtypeStruct((number * ROWS, LANES), jnp.float32)

    def chunked(number, chunks):
        return [pltpu.VMEM((number, rows, LANES), jnp.float32) for _ in range(HALVES) for _, rows in chunks]

    hbm = pl.BlockSpec(memory_space=pltpu.HBM)
    consts = [jnp.asarray(t) for t in tables()]

    def sems(number):
        return [pltpu.SemaphoreType.DMA((number,))] * 2

    return pl.pallas_call(
        exchange_kernel,
        out_shape=[
            *[out(SLC)] * HALVES,
            *[out(GRP)] * HALVES,
            jax.ShapeDtypeStruct((16, LANES), jnp.int32),
            jax.ShapeDtypeStruct((GRP, 1, LANES), jnp.int32),
        ],
        in_specs=[vmem, vmem, vmem, vmem, vmem, hbm, *[hbm] * len(consts)],
        out_specs=[vmem] * 6,
        scratch_shapes=[
            pltpu.VMEM(orb.shape, jnp.float32),
            pltpu.VMEM((ORB + 1, ROWS, LANES), jnp.float32),
            pltpu.VMEM((GRP, 1, LANES), jnp.int32),
            pltpu.SMEM((16, LANES), jnp.int32),
            pltpu.SMEM((GRP, 1, LANES), jnp.int32),
            *[pltpu.VMEM(t.shape, t.dtype) for t in consts],
            *[slots(SLC)] * (5 * HALVES),
            *chunked(GRP, CHUNKS),
            *chunked(GRP, CHUNKS),
            *chunked(SLC, CHUNKS),
            *chunked(SLC, BACK_CHUNKS),
            *chunked(GRP, BACK_CHUNKS),
            *[pltpu.VMEM((B, CELLS), jnp.float32)] * 2,
            pltpu.VMEM((2 * MARGIN + BLOCKS, B, LANES), jnp.float32),
            pltpu.VMEM((CELLS // 2 + PART - HELD, LANES), jnp.float32),
            pltpu.SemaphoreType.DMA((3,)),
            pltpu.SemaphoreType.DMA((len(consts),)),
            *sems(1),
            *sems(HALVES),
            *sems(HALVES),
            *sems(HALVES * N),
            *sems(HALVES * N),
            *sems(HALVES * N),
            *sems(HALVES * N),
        ],
        compiler_params=pltpu.CompilerParams(
            collective_id=0, has_side_effects=True, vmem_limit_bytes=VMEM_LIMIT
        ),
        name="exchange",
    )(owner, remote, resident, count, offsets, orb, *consts)


def sum_kernel(table, requested, *refs):
    hbm, out, total, held, sem = refs[:6], refs[6], refs[7], refs[8:14], refs[14]
    copies = [pltpu.make_async_copy(a, b, sem.at[n]) for n, (a, b) in enumerate(zip(hbm, held))]
    for copy in copies:
        copy.start()
    near, answers, (orb, pot) = held[:2], held[2:4], held[4:]
    total[...] = jnp.zeros_like(total)
    for h in range(HALVES):
        copies[h].wait()

        def add_near(t, _, h=h):
            total[part_of(table[NEAR, SLC * h + t], ROWS), :] += near[h][part_of(t, ROWS), :]
            return 0

        lax.fori_loop(0, SLC, add_near, 0, unroll=2)
    for h in range(HALVES):
        copies[HALVES + h].wait()

        def add_far(t, _, h=h):
            total[part_of(requested[t, 0, h], ROWS), :] += answers[h][part_of(t, ROWS), :]
            return 0

        lax.fori_loop(0, GRP, add_far, 0, unroll=2)
    for copy in copies[2 * HALVES :]:
        copy.wait()
    for q in range(BLOCKS):
        for p in range(PLANES):
            cols = slice(q * LANES, (q + 1) * LANES)
            field = total[pl.ds(3 * q + p, ORB, stride=ROWS), :]
            out[p, :, cols] = pot[p, :, cols] * orb[p, :, cols] - field


def sums(table, requested, orb, pot, fields):
    smem, vmem, hbm = (pl.BlockSpec(memory_space=m) for m in (pltpu.SMEM, pltpu.VMEM, pltpu.HBM))
    inputs = [*fields, orb, pot]
    return pl.pallas_call(
        sum_kernel,
        out_shape=jax.ShapeDtypeStruct(orb.shape, jnp.float32),
        in_specs=[smem, smem, *[hbm] * len(inputs)],
        out_specs=vmem,
        scratch_shapes=[
            pltpu.VMEM(((ORB + 1) * ROWS, LANES), jnp.float32),
            *[pltpu.VMEM(x.shape, jnp.float32) for x in inputs],
            pltpu.SemaphoreType.DMA((len(inputs),)),
        ],
        compiler_params=pltpu.CompilerParams(vmem_limit_bytes=VMEM_LIMIT),
        name="sums",
    )(table, requested, *inputs)


def per_device(orbitals, local_pot, pair_owner, pair_remote, pair_resident, pair_count, offsets):
    orb, pot = jnp.transpose(orbitals, (1, 0, 2)), jnp.transpose(local_pot, (1, 0, 2))
    *fields, table, requested = exchange(
        pair_owner.reshape(1, PAIRS), pair_remote, pair_resident, pair_count, offsets.T, orb
    )
    return jnp.transpose(sums(table, requested, orb, pot, fields), (1, 0, 2))


def solution(mesh):
    in_specs = (
        P("grp", "slc", None),
        P("grp", "slc", None),
        P("grp", None, None),
        P("grp", None),
        P("grp", None),
        P("grp", None),
        P(),
    )
    return jax.shard_map(
        per_device, mesh=mesh, in_specs=in_specs, out_specs=P("grp", "slc", None), check_vma=False
    )
```

```python
import functools

import jax
import jax.numpy as jnp
import numpy as np
from jax import lax
from jax.experimental import pallas as pl
from jax.experimental.pallas import tpu as pltpu
from jax.sharding import PartitionSpec as P

B = 48
CELLS = B * B
LANES = 128
BLOCKS = CELLS // LANES
PLANES = 3
ROWS = 56
GRP = 32
SLC = 16
ORB = 32
PAIRS = 32
HALVES = 2
CHUNKS = ((0, 40), (40, 14))
BACK_CHUNKS = ((0, 16), (16, 38))
MARGIN = 9
WIDE = 384
PART = 256
HELD = WIDE // 2
VMEM_LIMIT = 60 * 1024 * 1024

NEAR, OWNER, FAR, SEAT, WANT = 0, 1, 2, 3, 5
GAP, BLOCK, REST = 8, 11, 13


def split_np(values):
    high = values.astype(jnp.bfloat16)
    low = (values - high.astype(np.float64)).astype(jnp.bfloat16)
    return high, low


@functools.cache
def tables():
    k = np.arange(B, dtype=np.float64)
    q = np.sqrt(2.0 / (B + 1)) * np.sin(np.pi * np.outer(k + 1, k + 1) / (B + 1))
    lam = 2.0 - 2.0 * np.cos(np.pi * (k + 1) / (B + 1))
    plane_of = 3 * (np.arange(B) % SLC) + np.arange(B) // SLC
    q_c = np.zeros((WIDE, 2 * PART))
    for b in range(WIDE // B):
        for c in range(B):
            q_c[b * B : (b + 1) * B, PART * (c % 2) + b * (B // 2) + c // 2] = q[:, c]
    q_a = np.zeros((2 * B, LANES))
    q_a[:B, :B] = q[plane_of]
    q_a[B:, LANES // 2 : LANES // 2 + B] = q[plane_of]
    q_high, q_low = split_np(q)
    q_b = np.concatenate([q_high, q_low, q_high], axis=1)
    lam_b = np.broadcast_to(lam[:, None], (B, 2 * LANES)).astype(np.float32)
    lam_ac = np.ones((B // 4, 1, 2 * LANES), np.float32)
    for kc in range(B):
        start = (kc // 2 % 2) * LANES + (kc % 2) * (LANES // 2)
        lam_ac[kc // 4, 0, start : start + B] = lam + lam[kc]
    return (*split_np(q_c), *split_np(q_a), q_b, lam_b, lam_ac)


def iota(shape, dim):
    return lax.broadcasted_iota(jnp.int32, shape, dim)


def total_of(mask, values, axis):
    return jnp.sum(jnp.where(mask, values, 0), axis=axis, keepdims=True)


def index_tables(owner, remote, resident, count):
    square = (PAIRS, PAIRS)
    down, across = iota(square, 0), iota(square, 1)

    def as_column(row):
        return total_of(down == across, row, 1)

    owner_col = as_column(owner)
    same = owner_col == owner
    ones = jnp.ones(square, jnp.int32)

    def places(before, axis, other_axis):
        return total_of(same & before, ones, axis), total_of(same, ones, axis)

    rank_row, times_row = places(down < across, 0, 1)
    rank_col, times_col = places(across < down, 1, 0)

    def seats(rank, times, rank_other, times_other, before, axis):
        single, first, second = times == 1, (times == 2) & (rank == 0), rank == 1
        single_o, first_o, second_o = times_other == 1, (times_other == 2) & (rank_other == 0), rank_other == 1
        twice = jnp.sum(jnp.where(second_o, 1, 0), axis=axis, keepdims=True)
        at_first = total_of(before & first_o, ones, axis)
        at_second = total_of(before & second_o, ones, axis)
        filled = twice + total_of(before & single_o, ones, axis)
        late = single & (filled >= SLC)
        half = jnp.where(second | late, 1, 0)
        seat = jnp.where(
            first, at_first, jnp.where(second, at_second, jnp.where(late, filled - SLC + twice, filled))
        )
        return half, seat

    half_row, seat_row = seats(rank_row, times_row, rank_col, times_col, down < across, 0)
    half_col, seat_col = seats(rank_col, times_col, rank_row, times_row, across < down, 1)

    upto = iota((SLC, SLC), 1) <= iota((SLC, SLC), 0)
    running = total_of(upto, count, 1)
    home = jnp.sum(jnp.where(running <= iota((SLC, PAIRS), 1), 1, 0), axis=0, keepdims=True)
    near_col = as_column(home * 2 + resident)
    remote_col = as_column(remote)

    wide = (PAIRS, LANES)
    lane = iota(wide, 1)
    seated = (half_col * SLC + seat_col) == lane
    rows = [jnp.zeros((1, LANES), jnp.int32)] * 8
    rows[NEAR] = total_of(seated, near_col + jnp.zeros(wide, jnp.int32), 0)
    rows[OWNER] = total_of(seated, owner_col + jnp.zeros(wide, jnp.int32), 0)
    rows[FAR] = total_of(seated, owner_col * ORB + remote_col + jnp.zeros(wide, jnp.int32), 0)
    requests = jnp.zeros((GRP, LANES), jnp.int32)
    for h in range(HALVES):
        named = (owner_col == lane) & (half_col == h)
        rows[SEAT + h] = total_of(named, seat_col + jnp.zeros(wide, jnp.int32), 0)
        rows[WANT + h] = ORB + total_of(named, remote_col - ORB + jnp.zeros(wide, jnp.int32), 0)
        asked = (down == owner) & (half_row == h)
        want_col = ORB + total_of(asked, remote - ORB + jnp.zeros(square, jnp.int32), 1)
        requests = jnp.where(iota((GRP, LANES), 1) == h, want_col, requests)
    for n, most in ((NEAR, ORB - 1), (OWNER, GRP - 1), (SEAT, SLC - 1), (SEAT + 1, SLC - 1), (WANT, ORB), (WANT + 1, ORB)):
        rows[n] = jnp.clip(rows[n], 0, most)
    return rows, jnp.clip(requests, 0, ORB)


def shift_rows(rows, offsets, me_g, me_s):
    lane = iota((1, LANES), 1)
    orbital = iota(offsets.shape, 1)
    rows += [jnp.zeros((1, LANES), jnp.int32) for _ in range(8)]
    for h in range(HALVES):
        mine = lane == SLC * h + me_s
        near = me_g * ORB + total_of(mine, rows[NEAR], 1)
        far = total_of(mine, rows[FAR], 1)
        gap = total_of(orbital == near, offsets, 1) - total_of(orbital == far, offsets, 1)
        for k in range(3):
            rows[GAP + k] = jnp.where(lane == h, gap[k : k + 1], rows[GAP + k])
        turn = gap[1:2] * B + gap[2:3]
        for n, sign in enumerate((1, -1)):
            reach = sign * turn + MARGIN * LANES
            reach = jnp.clip(reach, 0, (2 * MARGIN) * LANES - 1)
            block = lax.div(reach, jnp.full_like(reach, LANES))
            rows[BLOCK + n] = jnp.where(lane == h, block, rows[BLOCK + n])
            rows[REST + n] = jnp.where(lane == h, reach - block * LANES, rows[REST + n])


def stack_rows(rows):
    at = iota((len(rows), LANES), 0)
    table = jnp.zeros((len(rows), LANES), jnp.int32)
    for n, row in enumerate(rows):
        table = jnp.where(at == n, row, table)
    return table


def split(values):
    high = values.astype(jnp.bfloat16)
    return high, (values - high.astype(jnp.float32)).astype(jnp.bfloat16)


def dot(left, right, dims=((1,), (0,))):
    return lax.dot_general(left, right, (dims, ((), ())), preferred_element_type=jnp.float32)


def plane_at(shape, dim):
    row = iota(shape, dim)
    return 3 * lax.rem(row, SLC) + lax.div(row, SLC)


GROUPS = [slice(g * WIDE, (g + 1) * WIDE) for g in range(CELLS // WIDE)]


def wire_places():
    for q in range(BLOCKS):
        for p in range(PLANES):
            yield (
                pl.ds(3 * q + p, SLC, stride=ROWS),
                slice(p * SLC, (p + 1) * SLC),
                slice(q * LANES, (q + 1) * LANES),
            )


def lane_shift(blocks, block, rest):
    loaded = [blocks[block + q] for q in range(BLOCKS + 1)]
    near, over = jnp.concatenate(loaded[:-1], axis=0), jnp.concatenate(loaded[1:], axis=0)
    high, low = split(jnp.concatenate([near, over], axis=1))
    square = (2 * LANES, LANES)
    onehot = jnp.where(iota(square, 0) == iota(square, 1) + rest, 1.0, 0.0).astype(jnp.bfloat16)
    out = dot(high, onehot) + dot(low, onehot)
    return jnp.concatenate([out[q * B : (q + 1) * B] for q in range(BLOCKS)], axis=1)


def pair_fields(gap, there, back, near_box, far_box, near_field, far_field, consts, scratch):
    qc_high, qc_low, qa_high, qa_low, q_b, lam_b, lam_ac = consts
    psi, moved, blocks, modes = scratch
    e0, e1, e2 = gap
    lane = iota((8, CELLS), 1)[:1]
    at_b, at_c = lax.div(lane, B) + e1, lax.rem(lane, B) + e2
    inside = (at_b >= 0) & (at_b < B) & (at_c >= 0) & (at_c < B)
    inside = jnp.where(inside, 1.0, 0.0).astype(jnp.float32)
    onehot = jnp.where(plane_at((B, B), 0) + e0 == plane_at((B, B), 1), 1.0, 0.0).astype(jnp.bfloat16)
    for where, rows, cols in wire_places():
        psi[rows, cols] = near_box[where, :]
        blocks[MARGIN + cols.start // LANES, rows, :] = far_box[where, :]
    high, low = split(lane_shift(blocks, *there) * inside)
    moved[...] = dot(onehot, high) + dot(onehot, low)

    density = jnp.concatenate([psi[:, cols] * moved[:, cols] for cols in GROUPS], axis=0)
    high, low = split(density)
    part = dot(high, qc_high[...]) + dot(low, qc_high[...]) + dot(high, qc_low[...])
    for g in range(len(GROUPS)):
        mine = part[g * B : (g + 1) * B]
        high, low = split(jnp.concatenate([mine[:, :PART], mine[:, PART:]], axis=0))
        over = ((0,), (0,))
        out = dot(high, qa_high[...], over) + dot(low, qa_high[...], over) + dot(high, qa_low[...], over)
        modes[g * HELD : (g + 1) * HELD, :] = out[:HELD]

    def along_b(values):
        high, low = split(values)
        return dot(q_b[...], jnp.concatenate([high, high, low], axis=0))

    def weigh(i, _):
        left, right = pl.ds(2 * i, B, stride=B // 2), pl.ds(2 * i + 1, B, stride=B // 2)
        values = along_b(jnp.concatenate([modes[left, :], modes[right, :]], axis=1))
        values = along_b(values / (lam_b[...] + lam_ac[i]))
        modes[left, :] = values[:, :LANES]
        modes[right, :] = values[:, LANES:]
        return 0

    lax.fori_loop(0, B // 4, weigh, 0, unroll=6)

    parts = []
    over = ((1,), (1,))
    for g in range(len(GROUPS)):
        high, low = split(modes[g * HELD : g * HELD + PART, :])
        out = dot(qa_high[...], high, over) + dot(qa_high[...], low, over) + dot(qa_low[...], high, over)
        parts.append(jnp.concatenate([out[:B], out[B:]], axis=1))
    high, low = split(jnp.concatenate(parts, axis=0))
    potential = dot(high, qc_high[...], over) + dot(low, qc_high[...], over) + dot(high, qc_low[...], over)
    for g, cols in enumerate(GROUPS):
        here = potential[g * B : (g + 1) * B]
        moved[:, cols] = here * moved[:, cols]
        high, low = split(here * psi[:, cols] * inside[:, cols])
        over = ((0,), (0,))
        apart = dot(onehot, high, over) + dot(onehot, low, over)
        for n in range(WIDE // LANES):
            blocks[MARGIN + cols.start // LANES + n] = apart[:, n * LANES : (n + 1) * LANES]
    far = lane_shift(blocks, *back)
    for where, rows, cols in wire_places():
        near_field[where, :] = moved[rows, cols]
        far_field[where, :] = far[rows, cols]


def peer(me, i, count):
    return lax.rem(me + (i // 2 + 1) * (1 - 2 * (i % 2)) + count, count)


def part_of(slot, count):
    return pl.ds(pl.multiple_of(slot * count, 8), count)


def rows_of(slot, row, count):
    return pl.ds(pl.multiple_of(slot * ROWS + row, 8), count)


N = len(CHUNKS)


def exchange_kernel(*refs):
    names = iter(refs)

    def take(count=1):
        out = [next(names) for _ in range(count)]
        return out[0] if count == 1 else out

    def halves():
        return take(HALVES)

    def chunked():
        return [take(N) for _ in range(HALVES)]

    owner, remote, resident, count_row, offsets, orb_hbm = take(6)
    consts_hbm = take(7)
    near_back, answers = halves(), halves()
    table_out, req_recv = take(2)
    orb, slabs, want, table_smem, req_smem = take(5)
    consts = take(7)
    near_send, near_box, far_box, near_field, far_field = (halves() for _ in range(5))
    g_send, g_recv, f_send, f_back, a_send = (chunked() for _ in range(5))
    scratch = take(4)
    local_sem, const_sem, own_sem, rq_s, rq_r, near_s, near_r, nback_s, nback_r = take(9)
    grp_s, grp_r, far_s, far_r, fback_s, fback_r, ans_s, ans_r = take(8)

    me_g, me_s = lax.axis_index("grp"), lax.axis_index("slc")

    def each(axis, action):
        me, count = (me_g, GRP) if axis == "grp" else (me_s, SLC)

        def step(i, _):
            action(peer(me, i, count))
            return 0

        lax.fori_loop(0, count - 1, step, 0, unroll=5 if axis == "slc" else 1)

    orb_copy = pltpu.make_async_copy(orb_hbm, orb, local_sem.at[2])
    orb_copy.start()
    const_copies = [pltpu.make_async_copy(a, b, const_sem.at[n]) for n, (a, b) in enumerate(zip(consts_hbm, consts))]
    for copy in const_copies:
        copy.start()
    barrier = pltpu.get_barrier_semaphore()
    each("grp", lambda there: pl.semaphore_signal(barrier, inc=1, device_id={"grp": there}))
    each("slc", lambda there: pl.semaphore_signal(barrier, inc=1, device_id={"slc": there}))

    rows, requests = index_tables(owner[...], remote[...], resident[...], count_row[...])
    shift_rows(rows, offsets[...], me_g, me_s)
    table_out[...] = stack_rows(rows)
    want[...] = requests.reshape(GRP, 1, LANES)
    local = pltpu.make_async_copy(table_out, table_smem, local_sem.at[0])
    local.start()
    orb_copy.wait()
    for q in range(BLOCKS):
        for p in range(PLANES):
            slabs[:ORB, 3 * q + p, :] = orb[p, :, q * LANES : (q + 1) * LANES]
    slabs[:ORB, 54:56, :] = jnp.zeros((ORB, 2, LANES), jnp.float32)
    slabs[ORB] = jnp.zeros((ROWS, LANES), jnp.float32)
    blocks = scratch[2]
    blocks[...] = jnp.zeros_like(blocks)
    scratch[3][CELLS // 2 :, :] = jnp.zeros((PART - HELD, LANES), jnp.float32)
    local.wait()
    pl.semaphore_wait(barrier, GRP + SLC - 2)

    def remote_copy(src, dst, send, recv, axis, there):
        return pltpu.make_async_remote_copy(
            src_ref=src, dst_ref=dst, send_sem=send, recv_sem=recv, device_id={axis: there}
        )

    def req_copy(there, slot):
        return remote_copy(want.at[there], req_recv.at[slot], rq_s.at[0], rq_r.at[0], "grp", there)

    def near_copy(h, there, slot):
        return remote_copy(
            near_send[h].at[part_of(there, ROWS)], near_box[h].at[part_of(slot, ROWS)],
            near_s.at[h], near_r.at[h], "slc", there,
        )

    def grp_copy(h, c, there, slot):
        return remote_copy(
            g_send[h][c].at[there], g_recv[h][c].at[slot], grp_s.at[N * h + c], grp_r.at[N * h + c], "grp", there
        )

    def far_copy(h, c, there, slot):
        row, count = CHUNKS[c]
        return remote_copy(
            f_send[h][c].at[there], far_box[h].at[rows_of(slot, row, count)],
            far_s.at[N * h + c], far_r.at[N * h + c], "slc", there,
        )

    def fback_copy(h, c, there, slot):
        row, count = BACK_CHUNKS[c]
        return remote_copy(
            far_field[h].at[rows_of(there, row, count)], f_back[h][c].at[slot],
            fback_s.at[N * h + c], fback_r.at[N * h + c], "slc", there,
        )

    def nback_copy(h, there, slot):
        return remote_copy(
            near_field[h].at[part_of(there, ROWS)], near_back[h].at[part_of(slot, ROWS)],
            nback_s.at[h], nback_r.at[h], "slc", there,
        )

    def ans_copy(h, c, there, slot):
        row, count = BACK_CHUNKS[c]
        return remote_copy(
            a_send[h][c].at[there], answers[h].at[rows_of(slot, row, count)],
            ans_s.at[N * h + c], ans_r.at[N * h + c], "grp", there,
        )

    def own_near(h):
        mine = part_of(me_s, ROWS)
        return pltpu.make_async_copy(near_field[h].at[mine], near_back[h].at[mine], own_sem.at[h])

    def own_answer(h, c):
        row, count = BACK_CHUNKS[c]
        there = answers[h].at[rows_of(me_g, row, count)]
        return pltpu.make_async_copy(a_send[h][c].at[me_g], there, own_sem.at[HALVES + N * h + c])

    def all_of(ref, size, send, recv, axis):
        me, count = (me_g, GRP) if axis == "grp" else (me_s, SLC)
        whole = ref.at[pl.ds(0, size)]
        return remote_copy(whole, whole, send, recv, axis, peer(me, 0, count))

    def all_req():
        return all_of(req_recv, GRP - 1, rq_s.at[0], rq_r.at[0], "grp")

    def all_near(h):
        return all_of(near_box[h], (SLC - 1) * ROWS, near_s.at[h], near_r.at[h], "slc")

    def all_grp(h, c):
        return all_of(g_recv[h][c], GRP - 1, grp_s.at[N * h + c], grp_r.at[N * h + c], "grp")

    def all_far(h, c):
        return all_of(f_send[h][c], SLC - 1, far_s.at[N * h + c], far_r.at[N * h + c], "slc")

    def all_fback(h, c):
        return all_of(f_back[h][c], SLC - 1, fback_s.at[N * h + c], fback_r.at[N * h + c], "slc")

    def all_nback(h):
        return all_of(near_back[h], (SLC - 1) * ROWS, nback_s.at[h], nback_r.at[h], "slc")

    def all_ans(h, c):
        return all_of(a_send[h][c], GRP - 1, ans_s.at[N * h + c], ans_r.at[N * h + c], "grp")

    def send_near(h):
        def one(there):
            near_send[h][part_of(there, ROWS), :] = slabs[table_smem[NEAR, SLC * h + there]]
            near_copy(h, there, me_s).start()

        each("slc", one)
        near_box[h][part_of(me_s, ROWS), :] = slabs[table_smem[NEAR, SLC * h + me_s]]

    def send_grp(h, c):
        row, count = CHUNKS[c]

        def one(there):
            g_send[h][c][there] = slabs[req_smem[there, 0, h], row : row + count, :]
            grp_copy(h, c, there, me_g).start()

        each("grp", one)
        g_recv[h][c][me_g] = slabs[table_smem[WANT + h, me_g], row : row + count, :]

    def forward_far(h, c):
        row, count = CHUNKS[c]
        all_grp(h, c).wait_recv()

        def one(there):
            f_send[h][c][there] = g_recv[h][c][table_smem[OWNER, SLC * h + there]]
            far_copy(h, c, there, me_s).start()

        each("slc", one)
        far_box[h][rows_of(me_s, row, count), :] = g_recv[h][c][table_smem[OWNER, SLC * h + me_s]]

    def compute(h):
        all_near(h).wait_recv()
        for c in range(N):
            all_far(h, c).wait_recv()
        gap = [table_smem[GAP + k, h] for k in range(3)]
        there, back = [(table_smem[BLOCK + n, h], table_smem[REST + n, h]) for n in range(2)]
        pair_fields(gap, there, back, near_box[h], far_box[h], near_field[h], far_field[h], consts, scratch)

    def send_fields(h):
        for c, (row, count) in enumerate(BACK_CHUNKS):
            each("slc", lambda there: fback_copy(h, c, there, me_s).start())
            f_back[h][c][me_s] = far_field[h][rows_of(me_s, row, count), :]

    def send_near_fields(h):
        each("slc", lambda there: nback_copy(h, there, me_s).start())
        own_near(h).start()

    def send_answers(h, c):
        row, count = BACK_CHUNKS[c]
        all_fback(h, c).wait_recv()

        def one(there):
            a_send[h][c][there] = f_back[h][c][table_smem[SEAT + h, there]]
            ans_copy(h, c, there, me_g).start()

        each("grp", one)
        a_send[h][c][me_g] = f_back[h][c][table_smem[SEAT + h, me_g]]
        own_answer(h, c).start()

    each("grp", lambda there: req_copy(there, me_g).start())
    req_recv[me_g] = want[me_g]
    send_near(0)
    all_req().wait_recv()
    asked = pltpu.make_async_copy(req_recv, req_smem, local_sem.at[1])
    asked.start()
    asked.wait()
    for c in range(N):
        send_grp(0, c)
    send_near(1)
    for c in range(N):
        forward_far(0, c)
        send_grp(1, c)
    for copy in const_copies:
        copy.wait()
    compute(0)
    send_fields(0)
    for c in range(N):
        forward_far(1, c)
        send_answers(0, c)
    send_near_fields(0)
    compute(1)
    send_fields(1)
    for c in range(N):
        send_answers(1, c)
    send_near_fields(1)

    all_req().wait_send()
    for h in range(HALVES):
        all_near(h).wait_send()
        all_nback(h).wait()
        own_near(h).wait()
        for c in range(N):
            all_grp(h, c).wait_send()
            all_far(h, c).wait_send()
            all_fback(h, c).wait_send()
            all_ans(h, c).wait()
            own_answer(h, c).wait()


def exchange(owner, remote, resident, count, offsets, orb):
    vmem = pl.BlockSpec(memory_space=pltpu.VMEM)

    def slots(number):
        return pltpu.VMEM((number * ROWS, LANES), jnp.float32)

    def out(number):
        return jax.ShapeDtypeStruct((number * ROWS, LANES), jnp.float32)

    def chunked(number, chunks):
        return [pltpu.VMEM((number, rows, LANES), jnp.float32) for _ in range(HALVES) for _, rows in chunks]

    hbm = pl.BlockSpec(memory_space=pltpu.HBM)
    consts = [jnp.asarray(t) for t in tables()]

    def sems(number):
        return [pltpu.SemaphoreType.DMA((number,))] * 2

    return pl.pallas_call(
        exchange_kernel,
        out_shape=[
            *[out(SLC)] * HALVES,
            *[out(GRP)] * HALVES,
            jax.ShapeDtypeStruct((16, LANES), jnp.int32),
            jax.ShapeDtypeStruct((GRP, 1, LANES), jnp.int32),
        ],
        in_specs=[vmem, vmem, vmem, vmem, vmem, hbm, *[hbm] * len(consts)],
        out_specs=[*[hbm] * (2 * HALVES), vmem, vmem],
        scratch_shapes=[
            pltpu.VMEM(orb.shape, jnp.float32),
            pltpu.VMEM((ORB + 1, ROWS, LANES), jnp.float32),
            pltpu.VMEM((GRP, 1, LANES), jnp.int32),
            pltpu.SMEM((16, LANES), jnp.int32),
            pltpu.SMEM((GRP, 1, LANES), jnp.int32),
            *[pltpu.VMEM(t.shape, t.dtype) for t in consts],
            *[slots(SLC)] * (5 * HALVES),
            *chunked(GRP, CHUNKS),
            *chunked(GRP, CHUNKS),
            *chunked(SLC, CHUNKS),
            *chunked(SLC, BACK_CHUNKS),
            *chunked(GRP, BACK_CHUNKS),
            *[pltpu.VMEM((B, CELLS), jnp.float32)] * 2,
            pltpu.VMEM((2 * MARGIN + BLOCKS, B, LANES), jnp.float32),
            pltpu.VMEM((CELLS // 2 + PART - HELD, LANES), jnp.float32),
            pltpu.SemaphoreType.DMA((3,)),
            pltpu.SemaphoreType.DMA((len(consts),)),
            pltpu.SemaphoreType.DMA((HALVES + HALVES * N,)),
            *sems(1),
            *sems(HALVES),
            *sems(HALVES),
            *sems(HALVES * N),
            *sems(HALVES * N),
            *sems(HALVES * N),
            *sems(HALVES * N),
        ],
        compiler_params=pltpu.CompilerParams(
            collective_id=0, has_side_effects=True, vmem_limit_bytes=VMEM_LIMIT
        ),
        name="exchange",
    )(owner, remote, resident, count, offsets, orb, *consts)


def sum_kernel(table, requested, *refs):
    hbm, out, total, held, sem = refs[:6], refs[6], refs[7], refs[8:14], refs[14]
    copies = [pltpu.make_async_copy(a, b, sem.at[n]) for n, (a, b) in enumerate(zip(hbm, held))]
    for copy in copies:
        copy.start()
    near, answers, (orb, pot) = held[:2], held[2:4], held[4:]
    total[...] = jnp.zeros_like(total)
    for h in range(HALVES):
        copies[h].wait()

        def add_near(t, _, h=h):
            total[part_of(table[NEAR, SLC * h + t], ROWS), :] += near[h][part_of(t, ROWS), :]
            return 0

        lax.fori_loop(0, SLC, add_near, 0, unroll=2)
    for h in range(HALVES):
        copies[HALVES + h].wait()

        def add_far(t, _, h=h):
            total[part_of(requested[t, 0, h], ROWS), :] += answers[h][part_of(t, ROWS), :]
            return 0

        lax.fori_loop(0, GRP, add_far, 0, unroll=2)
    for copy in copies[2 * HALVES :]:
        copy.wait()
    for q in range(BLOCKS):
        for p in range(PLANES):
            cols = slice(q * LANES, (q + 1) * LANES)
            field = total[pl.ds(3 * q + p, ORB, stride=ROWS), :]
            out[p, :, cols] = pot[p, :, cols] * orb[p, :, cols] - field


def sums(table, requested, orb, pot, fields):
    smem, vmem, hbm = (pl.BlockSpec(memory_space=m) for m in (pltpu.SMEM, pltpu.VMEM, pltpu.HBM))
    inputs = [*fields, orb, pot]
    return pl.pallas_call(
        sum_kernel,
        out_shape=jax.ShapeDtypeStruct(orb.shape, jnp.float32),
        in_specs=[smem, smem, *[hbm] * len(inputs)],
        out_specs=vmem,
        scratch_shapes=[
            pltpu.VMEM(((ORB + 1) * ROWS, LANES), jnp.float32),
            *[pltpu.VMEM(x.shape, jnp.float32) for x in inputs],
            pltpu.SemaphoreType.DMA((len(inputs),)),
        ],
        compiler_params=pltpu.CompilerParams(vmem_limit_bytes=VMEM_LIMIT),
        name="sums",
    )(table, requested, *inputs)


def per_device(orbitals, local_pot, pair_owner, pair_remote, pair_resident, pair_count, offsets):
    orb, pot = jnp.transpose(orbitals, (1, 0, 2)), jnp.transpose(local_pot, (1, 0, 2))
    *fields, table, requested = exchange(
        pair_owner.reshape(1, PAIRS), pair_remote, pair_resident, pair_count, offsets.T, orb
    )
    return jnp.transpose(sums(table, requested, orb, pot, fields), (1, 0, 2))


def solution(mesh):
    in_specs = (
        P("grp", "slc", None),
        P("grp", "slc", None),
        P("grp", None, None),
        P("grp", None),
        P("grp", None),
        P("grp", None),
        P(),
    )
    return jax.shard_map(
        per_device, mesh=mesh, in_specs=in_specs, out_specs=P("grp", "slc", None), check_vma=False
    )
```
